32 devices in a mesh: groups: 1, store: 32 (over z, y, x, core).
Axes of the slice: x: 2, y: 2, z: 4, core: 2. Of those that a mesh axis runs over, the one named last changes fastest.
Arguments:
- span_kv: bfloat16 [64, 512, 256], P(('groups', 'store')), may hold values from -6 to 6
- span_home: int32 [8], P('groups'), may hold values from 0 to 7, each once
- request_spans: int32 [32, 4], P('groups'), may hold values from 0 to 7, all different within a row
- recomp_pos: int32 [32, 4, 32], P('groups'), may hold values from 0 to 511, as said below
- new_q: bfloat16 [256, 130, 1024], P(('groups', 'store'))
- new_kv: bfloat16 [256, 130, 256], P(('groups', 'store'))
Outputs:
- attended: bfloat16 [256, 130, 1024], P(('groups', 'store'))
The draws below stay inside these ranges and needn't reach their ends.
Inputs may be any that keep to these rules, and one draw needn't show every extreme that they name: `span_home`: each span id is stored in exactly one slot. `request_spans`: a request names 4 different spans. `recomp_pos`: strictly increasing along the last dimension.
All inputs are finite; a program needn't handle non-finite values.
Results may differ from the reference program's by a relative error of at most 0.0087.
Values may be sent and summed in bfloat16 or wider, within the bound.
No kernel may reach another device: no remote copies, remote signals or barrier semaphores. Data moves between devices by JAX's collectives and lax.ppermute only.
A program may use at most 128 MiB of HBM per device.

```python
import jax
import jax.numpy as jnp
from jax import lax

KV_HEADS = 8
HD = 128
SPAN_LEN = 512
JOIN = 4
RECOMP = 32
CPG = 2
REQ_UNIT = 8
QPK = 8
SPANS = 8
REQUESTS = 32
ROWS = 130
STORE_ROWS = 64
N_STORE = 32


def draw_recomp_pos(key, part):
    key = jax.random.fold_in(key, 5)
    count = REQUESTS * JOIN
    row_keys = jax.random.split(key, count + 1)
    picks = jax.vmap(lambda one_key: jnp.sort(jax.random.permutation(one_key, SPAN_LEN)[:RECOMP]))(row_keys[:count])
    inner = jnp.sort(jax.random.permutation(row_keys[count], SPAN_LEN - 2)[:RECOMP - 2] + 1)
    first_row = jnp.concatenate([jnp.zeros((1,), jnp.int32), inner.astype(jnp.int32), jnp.full((1,), SPAN_LEN - 1, jnp.int32)])
    picks = picks.astype(jnp.int32).at[0].set(first_row)
    return picks.reshape(REQUESTS, JOIN, RECOMP).astype(jnp.int32)


def draw_new_kv(key, part):
    key = jax.random.fold_in(key, 11)
    shape = (N_STORE * REQ_UNIT, ROWS, 2 * HD)
    fresh = jax.random.normal(key, shape, jnp.float32)
    return fresh.astype(jnp.bfloat16)


def draw_new_q(key, part):
    key = jax.random.fold_in(key, 12)
    shape = (N_STORE * REQ_UNIT, ROWS, QPK * HD)
    queries = jax.random.normal(key, shape, jnp.float32)
    return queries.astype(jnp.bfloat16)


def levels(key, extent, cuts, low, high):
    loudness = 1.0
    for position, blocks in cuts:
        heights = jax.random.uniform(jax.random.fold_in(jax.random.fold_in(key, 6), position), (blocks,), jnp.float32, low / len(cuts), high / len(cuts))
        loudness = loudness * jnp.repeat(jnp.exp(heights), extent[position] // blocks).reshape((-1,) + (1,) * (len(extent) - 1 - position))
    return loudness


def choose_distinct(own_key, rows, amount, top, lift):
    sequence = jax.random.permutation(jax.random.fold_in(own_key, 1), amount)
    pull = sequence
    for power in range(3):
        pull = pull * pull // amount
    pull = pull * lift // amount
    lots = jax.random.randint(jax.random.fold_in(own_key, 2), (rows, amount), 0, 4096) + pull
    sure = jax.random.permutation(jax.random.fold_in(own_key, 3), rows)[jnp.arange(amount) % rows]
    lots = jnp.where(jnp.arange(rows)[:, None] == sure[None, :], 1 << 14, lots)
    score = lots * amount + jnp.arange(amount)
    return lax.top_k(score.astype(jnp.int32), top)[1].astype(jnp.int32)


def scatter_about(key, shape, deviation, bound, pieces=(), kind=jnp.bfloat16):
    values = jax.random.normal(key, shape, jnp.float32) * deviation
    if len(pieces) > 0:
        values = levels(key, shape, pieces, -0.22, 0.18) * values
    return jnp.clip(values, min=-bound, max=bound).astype(kind)


def setup_inputs(seed: int = 0, part: int = 0) -> dict:
    splits = jax.random.split(jax.random.key(seed), 7)
    part_splits = jax.random.split(jax.random.fold_in(splits[6], part), 7)
    span_kv = scatter_about(part_splits[0], (STORE_ROWS, SPAN_LEN, 2 * HD), 1.0, 6.0, ((0, 32),))
    span_home = jax.random.permutation(part_splits[1], SPANS).astype(jnp.int32)
    request_spans = choose_distinct(part_splits[2], REQUESTS, SPANS, JOIN, 8192)
    recomp_pos = draw_recomp_pos(jax.random.fold_in(jax.random.fold_in(splits[6], part), 71), part)
    new_q = draw_new_q(jax.random.fold_in(jax.random.fold_in(splits[6], part), 71), part)
    new_kv = draw_new_kv(jax.random.fold_in(jax.random.fold_in(splits[6], part), 71), part)
    return dict(span_kv=span_kv, span_home=span_home, request_spans=request_spans, recomp_pos=recomp_pos, new_q=new_q, new_kv=new_kv)


def rope_table(positions, half_dim):
    frequency = jnp.exp(-(2.0 * jnp.arange(half_dim).astype(jnp.float32) / (2.0 * half_dim)) * jnp.log(jnp.float32(500000.0)))
    angles = positions.astype(jnp.float32)[..., None] * frequency
    return (jnp.cos(angles), jnp.sin(angles))

def rotate(source_rows, cosines, sines):
    half_dim = source_rows.shape[-1] // 2
    front_half = source_rows[..., :half_dim]
    back_half = source_rows[..., half_dim:]
    return jnp.concatenate([front_half * cosines - back_half * sines, back_half * cosines + front_half * sines], -1)

def attend(cached, queries, fresh, offsets):
    joined_count, length, row_width = cached.shape
    head_dim = row_width // 2
    row_count = queries.shape[0]
    recomputed = joined_count * offsets.shape[1]
    decode_count = row_count - recomputed
    bases = jnp.arange(joined_count, dtype=jnp.int32) * length
    cosines, sines = rope_table(bases, head_dim // 2)
    key_rows = rotate(cached[..., :head_dim].astype(jnp.float32), cosines[:, None, :], sines[:, None, :])
    key_rows = key_rows.astype(jnp.bfloat16).reshape(joined_count * length, head_dim)
    value_rows = cached[..., head_dim:].reshape(joined_count * length, head_dim)
    places = (offsets + bases[:, None]).reshape(-1).astype(jnp.int32)
    row_pos = jnp.concatenate([places, joined_count * length + jnp.arange(decode_count, dtype=jnp.int32)])
    row_cos, row_sin = rope_table(row_pos, head_dim // 2)
    fresh_keys = rotate(fresh[:, :head_dim].astype(jnp.float32), row_cos, row_sin).astype(jnp.bfloat16)
    fresh_values = fresh[:, head_dim:]
    key_rows = key_rows.at[places].set(fresh_keys[:recomputed])
    value_rows = value_rows.at[places].set(fresh_values[:recomputed])
    key_rows = jnp.concatenate([key_rows, fresh_keys[recomputed:]], 0)
    value_rows = jnp.concatenate([value_rows, fresh_values[recomputed:]], 0)
    head_count = queries.shape[1] // head_dim
    query_rows = queries.reshape(row_count, head_count, head_dim).astype(jnp.float32)
    query_rows = rotate(query_rows, row_cos[:, None, :], row_sin[:, None, :]).astype(jnp.bfloat16)
    scores = jnp.einsum('rhd,kd->hrk', query_rows.astype(jnp.float32), key_rows.astype(jnp.float32)) / jnp.sqrt(jnp.float32(head_dim))
    key_pos = jnp.arange(key_rows.shape[0], dtype=jnp.int32)
    visible = key_pos[None, None, :] <= row_pos[None, :, None]
    scores = jnp.where(visible, scores, jnp.float32(-1e+30))
    peaks = lax.optimization_barrier(jnp.max(scores, -1, keepdims=True))
    powers = jnp.where(visible, jnp.exp(scores - peaks), jnp.float32(0.0))
    totals = lax.optimization_barrier(jnp.sum(powers, -1, keepdims=True))
    weights = (powers / totals).astype(jnp.bfloat16)
    output = jnp.einsum('hrk,kd->rhd', weights.astype(jnp.float32), value_rows.astype(jnp.float32))
    return output.reshape(row_count, head_count * head_dim).astype(jnp.bfloat16)

def reference(span_kv, span_home, request_spans, recomp_pos, new_q, new_kv):

    def single(unit_index):
        unit_block = unit_index // REQ_UNIT
        member = unit_index % REQ_UNIT
        store_group = unit_block // KV_HEADS
        kv_head = unit_block % KV_HEADS
        request = store_group * REQ_UNIT + member
        span_slots = span_home[request_spans[request]]
        store_rows = (span_slots // CPG * KV_HEADS + kv_head) * CPG + span_slots % CPG
        cached = span_kv[store_rows.astype(jnp.int32)]
        return attend(cached, new_q[unit_index], new_kv[unit_index], recomp_pos[request])
    return lax.map(single, jnp.arange(new_q.shape[0], dtype=jnp.int32))
```

```python
import functools
import math

import jax
import jax.numpy as jnp
from jax import lax
from jax.experimental import pallas as pl
from jax.experimental.pallas import tpu as pltpu
from jax.sharding import PartitionSpec as P

KV_HEADS = 8
LOG2E = 1.4426950408889634
BIG = 2.0**100
MIB = 1 << 20
SINE = (6.283185272447939, -41.34169703819957, 81.60502363802357, -76.7015376701132,
        42.01607576102491, -14.868322748754837, 3.1993388405088488)


def shifted(value, axis, by):
    devices = lax.axis_size(axis)
    return lax.ppermute(value, axis, [(i, (i + by) % devices) for i in range(devices)])


def sine_of_turns(t):
    r = t - jnp.floor(t + 0.5)
    square = r * r
    value = jnp.full(r.shape, SINE[-1], jnp.float32)
    for coefficient in SINE[-2::-1]:
        value = value * square + coefficient
    return value * r


def turns_per_step(index, dim):
    return jnp.exp(-(2.0 / dim) * math.log(500000.0) * index.astype(jnp.float32)) * (0.5 / math.pi)


def turn(rows, cosines, sines):
    return rows * cosines + pltpu.roll(rows, rows.shape[-1] // 2, 1) * sines


class Plan:
    def __init__(self, span_kv, request_spans, recomp_pos, new_q, groups):
        self.groups = groups
        self.per_group, self.length, width = span_kv.shape
        self.dim = width // 2
        self.piece = 2 * self.dim
        self.join = request_spans.shape[1]
        self.fresh = recomp_pos.shape[2]
        self.requests, self.rows, query_width = new_q.shape
        self.heads = query_width // self.dim
        self.recomputed = self.join * self.fresh
        self.decode = self.rows - self.recomputed
        self.block = self.heads * self.fresh
        self.tail = self.heads * self.decode
        self.height = self.join * self.block + self.tail
        self.slots = groups * self.per_group


def pack_kernel(plan, spans, *outs):
    dim, piece = plan.dim, plan.piece
    for s in range(plan.per_group):
        for first in range(0, plan.length, piece):
            keys = spans[s, first : first + piece, :dim].astype(jnp.float32)
            outs[s][first : first + dim, :] = keys.T.astype(jnp.bfloat16)
            outs[s][first + dim : first + piece, :dim] = spans[s, first : first + dim, dim:]
            outs[s][first + dim : first + piece, dim:] = spans[s, first + dim : first + piece, dim:]


def plan_work(plan, me, home, spans, work):
    stride = plan.requests + 1
    for chunk in range(plan.slots):
        for i in range(stride):
            work[chunk * stride + i] = 0
    for u in range(plan.requests):
        for j in range(plan.join):
            slot = home[spans[j, me[0] * plan.requests + u]]
            group = lax.div(slot, plan.per_group)
            distance = lax.rem(group - me[0] + plan.groups, plan.groups)
            chunk = distance * plan.per_group + slot - group * plan.per_group
            count = work[chunk * stride] + 1
            work[chunk * stride] = count
            work[chunk * stride + count] = u * plan.join + j
            work[plan.slots * stride + u * plan.join + j] = chunk


def prepare_kernel(plan, me, home, spans, newq_hbm, newkv_hbm, recomp, q_out, acc, places, turns, marks, fresh_k, fresh_v,
                   last_kv, work, tok, newq, newkv, table, flat, tails, column, mask, sems):
    loads = [pltpu.make_async_copy(newq_hbm, newq, sems.at[0]), pltpu.make_async_copy(newkv_hbm, newkv, sems.at[1])]
    for load in loads:
        load.start()
    plan_work(plan, me, home, spans, work)
    dim, fresh, requests, heads, block = plan.dim, plan.fresh, plan.requests, plan.heads, plan.block
    recomputed, decode, join = plan.recomputed, plan.decode, plan.join
    half = dim // 2
    scale = LOG2E / (dim**0.5)
    tok[...] = jnp.zeros(tok.shape, jnp.float32)

    row = lax.broadcasted_iota(jnp.int32, (dim, dim), 0)
    rate = turns_per_step(lax.rem(row, half), dim)
    phase = jnp.where(row < half, 0.25, 0.0)
    for j in range(join):
        turns[j] = sine_of_turns(rate * float(j * plan.length) + phase)

    row = lax.broadcasted_iota(jnp.int32, (plan.height, dim), 0)
    lane = lax.broadcasted_iota(jnp.int32, (plan.height, dim), 1)
    counts = ((lane >= fresh) & (lane < 2 * fresh)) | ((row < block) & (lane == lax.rem(row, fresh)))
    marks[...] = jnp.where(counts, 1.0, 0.0).astype(jnp.bfloat16)

    row = lax.broadcasted_iota(jnp.int32, (plan.height, recomputed), 0)
    key = lax.broadcasted_iota(jnp.int32, (plan.height, recomputed), 1)
    reach = (row // block) * fresh + lax.rem(row, fresh)
    mask[...] = jnp.where((row >= join * block) | (key <= reach), 0.0, -BIG)

    lane = lax.broadcasted_iota(jnp.int32, (fresh, dim), 1)
    rate = turns_per_step(lax.rem(lane, half), dim)
    signed = jnp.where(lane < half, -rate, rate)

    def places_of(u, carry):
        request = me[0] * requests + u
        column[:join, :fresh] = recomp[request].astype(jnp.float32)
        upright = column[...].T
        for j in range(join):
            inside = jnp.broadcast_to(upright[:fresh, j : j + 1], (fresh, dim))
            places[u * join + j] = inside
            at = inside + float(j * plan.length)
            table[0, u, j * fresh : (j + 1) * fresh, :] = sine_of_turns(at * rate + 0.25)
            table[1, u, j * fresh : (j + 1) * fresh, :] = sine_of_turns(at * signed)
        return carry

    column[...] = jnp.zeros(column.shape, jnp.float32)
    lax.fori_loop(0, requests, places_of, 0)
    step = lax.broadcasted_iota(jnp.int32, (decode * requests, dim), 0) // requests
    at = (join * plan.length + step).astype(jnp.float32)
    lane = lax.broadcasted_iota(jnp.int32, (decode * requests, dim), 1)
    rate = turns_per_step(lax.rem(lane, half), dim)
    last_cos = sine_of_turns(at * rate + 0.25)
    last_sin = sine_of_turns(at * jnp.where(lane < half, -rate, rate))

    for load in loads:
        load.wait()

    def queries_of(j, carry):
        rows = pl.ds(pl.multiple_of(j * fresh, fresh), fresh)
        for head in range(heads):
            x = newq[rows, :, head * dim : (head + 1) * dim].astype(jnp.float32)
            flat[head, : fresh * requests, :] = x.reshape(fresh * requests, dim)
        for u in range(requests):
            cosines = table[0, u, rows, :] * scale
            sines = table[1, u, rows, :] * scale
            for head in range(heads):
                y = turn(flat[head, pl.ds(u, fresh, stride=requests), :], cosines, sines)
                q_out[u, pl.ds(pl.multiple_of(j * block + head * fresh, fresh), fresh), :] = y.astype(jnp.bfloat16)
        return carry

    lax.fori_loop(0, join, queries_of, 0)
    for head in range(heads):
        x = newq[recomputed:, :, head * dim : (head + 1) * dim].astype(jnp.float32)
        y = turn(x.reshape(decode * requests, dim), last_cos, last_sin) * scale
        tails[head * decode * requests : (head + 1) * decode * requests, :] = y
    for u in range(requests):
        y = tails[pl.ds(u, plan.tail, stride=requests), :]
        q_out[u, join * block :, :] = y.astype(jnp.bfloat16)

    x = newkv[:recomputed, :, :].astype(jnp.float32)
    for side in range(2):
        flat[side] = x[:, :, side * dim : (side + 1) * dim].reshape(recomputed * requests, dim)
    x = newkv[recomputed:, :, :].astype(jnp.float32)
    last_kv[:, :dim] = turn(x[:, :, :dim].reshape(decode * requests, dim), last_cos, last_sin).astype(
        jnp.bfloat16
    ).astype(jnp.float32)
    last_kv[:, dim:] = x[:, :, dim:].reshape(decode * requests, dim)
    ones = jnp.ones((recomputed, dim), jnp.bfloat16)
    which = lax.rem(lax.broadcasted_iota(jnp.int32, (plan.tail, dim), 0), decode)

    def fresh_of(u, carry):
        y = turn(flat[0, pl.ds(u, recomputed, stride=requests), :], table[0, u], table[1, u])
        fresh_k[u] = y.T.astype(jnp.bfloat16)
        fresh_v[u] = flat[1, pl.ds(u, recomputed, stride=requests), :].astype(jnp.bfloat16)
        s = jnp.dot(q_out[u], fresh_k[u], preferred_element_type=jnp.float32)
        p = jnp.exp2(s + mask[...]).astype(jnp.bfloat16)
        values = jnp.concatenate([fresh_v[u], ones], 1)
        acc[u] = jnp.dot(p, values, preferred_element_type=jnp.float32)
        mine = q_out[u, join * block :, :].astype(jnp.float32)
        for d in range(decode):
            pair = last_kv[pl.ds(d * requests + u, 1), :]
            s = jnp.sum(mine * pair[:, :dim], 1, keepdims=True)
            p = jnp.where(which >= d, jnp.exp2(jnp.broadcast_to(s, which.shape)), 0.0)
            p = p.astype(jnp.bfloat16).astype(jnp.float32)
            acc[u, join * block :, :dim] += p * pair[:, dim:]
            acc[u, join * block :, dim:] += p
        return carry

    lax.fori_loop(0, requests, fresh_of, 0)


def spread_chunk(plan, chunk, values):
    dim, piece = plan.dim, plan.piece
    for first in range(0, chunk.shape[0], piece):
        values[first : first + dim, :dim] = chunk[first + dim : first + piece, :dim]
        values[first + dim : first + piece, :dim] = chunk[first + dim : first + piece, dim:]


def shift_keys(plan, chunk, first_token, place, angles, keys):
    dim, piece, fresh = plan.dim, plan.piece, plan.fresh
    half = dim // 2
    wide = lambda x: jnp.concatenate([x] * (piece // dim), 1)
    cosines, sines = wide(angles[:half]), wide(angles[half:])
    place = wide(place)
    for first in range(0, chunk.shape[0], piece):
        columns = slice(first, first + piece)
        a = chunk[first : first + half, :].astype(jnp.float32)
        b = chunk[first + half : first + dim, :].astype(jnp.float32)
        keys[:half, columns] = (a * cosines - b * sines).astype(jnp.bfloat16)
        keys[half:dim, columns] = (b * cosines + a * sines).astype(jnp.bfloat16)
        token = lax.broadcasted_iota(jnp.int32, (fresh, piece), 1) + (first_token + first)
        token = token.astype(jnp.float32)
        keys[dim : dim + fresh, columns] = jnp.where(token > place, -BIG, 0.0).astype(jnp.bfloat16)
        keys[dim + fresh : dim + 2 * fresh, columns] = jnp.where(token == place, -BIG, 0.0).astype(jnp.bfloat16)


def chunk_kernel(plan, order, work, chunk, places, turns, marks, q, _, acc, tok, keys, values):
    dim, block, join = plan.dim, plan.block, plan.join
    tok[...] = jnp.zeros(tok.shape, jnp.float32)
    length = chunk.shape[0]
    keys[dim + 2 * plan.fresh :, :] = jnp.zeros((dim - 2 * plan.fresh, length), jnp.bfloat16)
    values[:, dim:] = jnp.ones((length, dim), jnp.bfloat16)
    spread_chunk(plan, chunk, values)
    base = order * (plan.requests + 1)

    def prepare(n):
        place = work[base + 1 + n]
        shift_keys(plan, chunk, 0, places[place], turns[lax.rem(place, join)], keys)

    def one(n, carry):
        place = work[base + 1 + n]
        u = lax.div(place, join)
        j = place - u * join
        for k in range(join):

            @pl.when(j == k)
            def _():
                count = plan.height - k * block
                left = jnp.concatenate([q[u, k * block :, :], marks[:count, :]], 1)
                s = jnp.dot(left, keys[...], preferred_element_type=jnp.float32)
                prepare(jnp.minimum(n + 1, plan.requests - 1))
                p = jnp.exp2(s).astype(jnp.bfloat16)
                acc[u, k * block :, :] += jnp.dot(p, values[...], preferred_element_type=jnp.float32)

        return carry

    prepare(0)
    lax.fori_loop(0, work[base], one, 0)


def finish_kernel(plan, work, *refs):
    chunks = refs[: plan.slots]
    (places, turns, marks, q, acc, fresh_k, fresh_v, last_kv, out,
     done, flat, tails, joined, keys, values, top, total, peak, sems, load) = refs[plan.slots :]
    dim, fresh, requests, heads, block = plan.dim, plan.fresh, plan.requests, plan.heads, plan.block
    recomputed, decode, join = plan.recomputed, plan.decode, plan.join

    def put(u, source, seen):
        least, most, odd = seen
        for head in range(heads):
            rows = slice(head * fresh, (head + 1) * fresh)
            a, weight = source(rows)
            o = a / weight
            least, most = jnp.minimum(least, weight), jnp.maximum(most, weight)
            odd = odd + o * 0.0
            flat[head, pl.ds(u, fresh, stride=requests), :] = o
        return least, most, odd

    def put_tail(u, a, weight):
        o = a / weight
        tails[pl.ds(u, plan.tail, stride=requests), :] = o
        return weight, weight, o * 0.0

    def write(j):
        rows = pl.ds(j * fresh, fresh)
        for head in range(heads):
            x = flat[head].reshape(fresh, requests, dim)
            done[rows, :, head * dim : (head + 1) * dim] = x.astype(jnp.bfloat16)
        return rows

    def write_tail():
        for head in range(heads):
            x = tails[head * decode * requests : (head + 1) * decode * requests, :]
            done[recomputed:, :, head * dim : (head + 1) * dim] = x.reshape(decode, requests, dim).astype(jnp.bfloat16)

    def send(j):
        rows = pl.ds(j * fresh, fresh) if j < join else pl.ds(recomputed, decode)
        return pltpu.make_async_copy(done.at[rows], out.at[rows], sems.at[j])

    shape = (fresh, dim)
    seen = (jnp.full(shape, 1.0, jnp.float32), jnp.full(shape, 1.0, jnp.float32), jnp.zeros(shape, jnp.float32))
    tail_good = jnp.bool_(True)
    for u in range(requests):
        a = acc[u, join * block :, :]
        least, most, odd = put_tail(u, a[:, :dim], a[:, dim:])
        tail_good &= (jnp.min(least) > 2.0**-60) & (jnp.max(most) < 2.0**60) & (jnp.min(odd) == 0.0)
    write_tail()
    send(join).start()
    for j in range(join):
        for u in range(requests):
            source = lambda rows: (
                acc[u, j * block + rows.start : j * block + rows.stop, :dim],
                acc[u, j * block + rows.start : j * block + rows.stop, dim:],
            )
            seen = put(u, source, seen)
        write(j)
        send(j).start()
    least, most, odd = seen
    good = tail_good & (jnp.min(least) > 2.0**-60) & (jnp.max(most) < 2.0**60) & (jnp.min(odd) == 0.0)
    for j in range(join + 1):
        send(j).wait()

    @pl.when(jnp.logical_not(good))
    def _():
        keys[dim + 2 * fresh :, :] = jnp.zeros((dim - 2 * fresh, plan.length), jnp.bfloat16)
        unseen = (jnp.full(shape, 1.0, jnp.float32), jnp.full(shape, 1.0, jnp.float32), jnp.zeros(shape, jnp.float32))

        def fold(rows, s, v):
            before = peak[rows, :]
            now = jnp.maximum(before, jnp.max(s, 1, keepdims=True))
            peak[rows, :] = now
            fade = jnp.exp2(before - now)
            p = jnp.exp2(s - now[:, :1]).astype(jnp.bfloat16)
            total[rows, :] = total[rows, :] * fade + jnp.sum(p.astype(jnp.float32), 1, keepdims=True)
            top[rows, :] = top[rows, :] * fade + jnp.dot(p, v, preferred_element_type=jnp.float32)

        def sums(u, j):
            count = block if j < join else plan.tail
            every = pl.ds(0, count)
            peak[every, :] = jnp.full((count, dim), -3.0e38, jnp.float32)
            top[every, :] = jnp.zeros((count, dim), jnp.float32)
            total[every, :] = jnp.zeros((count, dim), jnp.float32)
            mine = q[u, j * block : j * block + count, :]
            s = jnp.dot(mine, fresh_k[u], preferred_element_type=jnp.float32)
            key = lax.broadcasted_iota(jnp.int32, s.shape, 1)
            row = lax.broadcasted_iota(jnp.int32, s.shape, 0)
            if j < join:
                s = jnp.where(key <= j * fresh + lax.rem(row, fresh), s, -BIG)
            fold(every, s, fresh_v[u])
            for k in range(min(j + 1, join)):
                for order, chunk in enumerate(chunks):

                    @pl.when(work[plan.slots * (requests + 1) + u * join + k] == order)
                    def _():
                        copy = pltpu.make_async_copy(chunk, joined, load.at[0])
                        copy.start()
                        copy.wait()

                spread_chunk(plan, joined, values)
                shift_keys(plan, joined, 0, places[u * join + k], turns[k], keys)
                mark = marks[:count, :] if k == j else marks[block : block + count, :]
                left = jnp.concatenate([mine, mark], 1)
                s = jnp.dot(left, keys[...], preferred_element_type=jnp.float32)
                fold(every, s, values[:, :dim])
            if j == join:
                which = lax.rem(lax.broadcasted_iota(jnp.int32, (count, dim), 0), decode)
                for d in range(decode):
                    pair = last_kv[pl.ds(d * requests + u, 1), :]
                    s = jnp.sum(mine.astype(jnp.float32) * pair[:, :dim], 1, keepdims=True)
                    s = jnp.where(which >= d, s, -BIG)
                    before = peak[every, :]
                    now = jnp.maximum(before, s)
                    peak[every, :] = now
                    p = jnp.exp2(s - now)
                    total[every, :] = total[every, :] * jnp.exp2(before - now) + p
                    top[every, :] = top[every, :] * jnp.exp2(before - now) + p * pair[:, dim:]

        for j in range(join + 1):

            def again(u, carry):
                sums(u, j)
                if j < join:
                    put(u, lambda rows: (top[rows, :], total[rows, :]), unseen)
                else:
                    put_tail(u, top[: plan.tail, :], total[: plan.tail, :])
                return carry

            lax.fori_loop(0, requests, again, 0)
            if j < join:
                write(j)
            else:
                write_tail()
            copy = send(j)
            copy.start()
            copy.wait()


def local(span_kv, span_home, request_spans, recomp_pos, new_q, new_kv):
    groups = lax.axis_size("store") // KV_HEADS
    me = (lax.axis_index("store") // KV_HEADS).reshape(1).astype(jnp.int32)
    plan = Plan(span_kv, request_spans, recomp_pos, new_q, groups)
    dim, join, requests = plan.dim, plan.join, plan.requests
    vmem = pl.BlockSpec(memory_space=pltpu.VMEM)
    smem = pl.BlockSpec(memory_space=pltpu.SMEM)
    anywhere = pl.BlockSpec(memory_space=pl.ANY)
    params = lambda mib: pltpu.CompilerParams(vmem_limit_bytes=mib * MIB)
    inside = lambda x: pltpu.with_memory_space_constraint(x, pltpu.VMEM)
    outside = lambda x: pltpu.with_memory_space_constraint(x, pltpu.HBM)
    cost = lambda us: pl.CostEstimate(flops=int(us * 1.1e9), bytes_accessed=0, transcendentals=0)

    packed = pl.pallas_call(
        functools.partial(pack_kernel, plan),
        out_shape=[pltpu.VMEM((plan.length, 2 * dim), jnp.bfloat16)] * plan.per_group,
        in_specs=[vmem],
        out_specs=[vmem] * plan.per_group,
        compiler_params=params(6),
        cost_estimate=cost(1.0),
        name="pack",
    )(span_kv)

    moving = [shifted(x, "store", -KV_HEADS) for x in packed] if groups > 1 else []

    spans = request_spans.T

    token = pltpu.VMEM((8, 128), jnp.float32)
    acc_type = pltpu.VMEM((requests, plan.height, 2 * dim), jnp.float32)
    q, acc, places, turns, marks, fresh_k, fresh_v, last_kv, work, tok = pl.pallas_call(
        functools.partial(prepare_kernel, plan),
        out_shape=[
            pltpu.VMEM((requests, plan.height, dim), jnp.bfloat16),
            acc_type,
            pltpu.VMEM((requests * join, plan.fresh, dim), jnp.float32),
            pltpu.VMEM((join, dim, dim), jnp.float32),
            pltpu.VMEM((plan.height, dim), jnp.bfloat16),
            pltpu.VMEM((requests, dim, plan.recomputed), jnp.bfloat16),
            pltpu.VMEM((requests, plan.recomputed, dim), jnp.bfloat16),
            pltpu.VMEM((plan.decode * requests, 2 * dim), jnp.float32),
            pltpu.SMEM((plan.slots * (requests + 1) + requests * join,), jnp.int32),
            token,
        ],
        in_specs=[smem] * 3 + [anywhere] * 2 + [vmem],
        out_specs=[vmem] * 8 + [smem, vmem],
        scratch_shapes=[
            pltpu.VMEM((plan.rows, requests, new_q.shape[2]), jnp.bfloat16),
            pltpu.VMEM((plan.rows, requests, 2 * dim), jnp.bfloat16),
            pltpu.VMEM((2, requests, plan.recomputed, dim), jnp.float32),
            pltpu.VMEM((plan.heads, plan.recomputed * requests, dim), jnp.float32),
            pltpu.VMEM((plan.heads * plan.decode * requests, dim), jnp.float32),
            pltpu.VMEM((dim, dim), jnp.float32),
            pltpu.VMEM((plan.height, plan.recomputed), jnp.float32),
            pltpu.SemaphoreType.DMA((2,)),
        ],
        compiler_params=params(20),
        cost_estimate=cost(6.0),
        name="prepare",
    )(me, span_home, spans, outside(new_q.transpose(1, 0, 2)), outside(new_kv.transpose(1, 0, 2)), recomp_pos)
    work = pltpu.with_memory_space_constraint(work, pltpu.SMEM)

    def take(order, chunk, acc):
        return pl.pallas_call(
            functools.partial(chunk_kernel, plan, order),
            out_shape=[acc_type, token],
            in_specs=[smem] + [vmem] * 6,
            out_specs=[vmem] * 2,
            input_output_aliases={6: 0},
            scratch_shapes=[
                pltpu.VMEM((2 * dim, plan.length), jnp.bfloat16),
                pltpu.VMEM((plan.length, 2 * dim), jnp.bfloat16),
            ],
            compiler_params=params(12),
            cost_estimate=cost(2.5),
            name="chunk",
        )(work, *map(inside, [chunk, places, turns, marks, q, acc]))

    def onward(k, tok):
        if k + plan.per_group < plan.slots - plan.per_group:
            held, tok = lax.optimization_barrier((buffers[plan.per_group + k], tok))
            buffers.append(shifted(held, "store", -KV_HEADS))

    buffers = list(packed) + moving
    onward(0, tok)
    for order in range(plan.slots):
        acc, tok = take(order, buffers[order], acc)
        if order < plan.per_group - 1:
            onward(order + 1, tok)
        elif order >= plan.per_group:
            onward(order, tok)

    out = pl.pallas_call(
        functools.partial(finish_kernel, plan),
        out_shape=jax.ShapeDtypeStruct((plan.rows, requests, new_q.shape[2]), jnp.bfloat16),
        in_specs=[smem] + [anywhere] * len(buffers) + [vmem] * 8,
        out_specs=anywhere,
        scratch_shapes=[
            pltpu.VMEM((plan.rows, requests, new_q.shape[2]), jnp.bfloat16),
            pltpu.VMEM((plan.heads, plan.fresh * requests, dim), jnp.float32),
            pltpu.VMEM((plan.heads * plan.decode * requests, dim), jnp.float32),
            pltpu.VMEM((plan.length, 2 * dim), jnp.bfloat16),
            pltpu.VMEM((2 * dim, plan.length), jnp.bfloat16),
            pltpu.VMEM((plan.length, 2 * dim), jnp.bfloat16),
            pltpu.VMEM((plan.block, dim), jnp.float32),
            pltpu.VMEM((plan.block, dim), jnp.float32),
            pltpu.VMEM((plan.block, dim), jnp.float32),
            pltpu.SemaphoreType.DMA((join + 1,)),
            pltpu.SemaphoreType.DMA((1,)),
        ],
        compiler_params=params(24),
        cost_estimate=cost(3.0),
        name="finish",
    )(work, *buffers, *map(inside, [places, turns, marks, q, acc, fresh_k, fresh_v, last_kv]))
    return out.transpose(1, 0, 2)


def solution(mesh):
    return jax.shard_map(
        local,
        mesh=mesh,
        in_specs=(
            P(("groups", "store"), None, None),
            P("groups"),
            P("groups", None),
            P("groups", None, None),
            P(("groups", "store"), None, None),
            P(("groups", "store"), None, None),
        ),
        out_specs=P(("groups", "store"), None, None),
        check_vma=False,
    )
```

```python
import functools
import math

import jax
import jax.numpy as jnp
from jax import lax
from jax.experimental import pallas as pl
from jax.experimental.pallas import tpu as pltpu
from jax.sharding import PartitionSpec as P

KV_HEADS = 8
LOG2E = 1.4426950408889634
BIG = 2.0**100
MIB = 1 << 20
SINE = (6.283185272447939, -41.34169703819957, 81.60502363802357, -76.7015376701132,
        42.01607576102491, -14.868322748754837, 3.1993388405088488)


def shifted(value, axis, by):
    devices = lax.axis_size(axis)
    return lax.ppermute(value, axis, [(i, (i + by) % devices) for i in range(devices)])


def sine_of_turns(t):
    r = t - jnp.floor(t + 0.5)
    square = r * r
    value = jnp.full(r.shape, SINE[-1], jnp.float32)
    for coefficient in SINE[-2::-1]:
        value = value * square + coefficient
    return value * r


def turns_per_step(index, dim):
    return jnp.exp(-(2.0 / dim) * math.log(500000.0) * index.astype(jnp.float32)) * (0.5 / math.pi)


def turn(rows, cosines, sines):
    return rows * cosines + pltpu.roll(rows, rows.shape[-1] // 2, 1) * sines


class Plan:
    def __init__(self, span_kv, request_spans, recomp_pos, new_q, groups):
        self.groups = groups
        self.per_group, self.length, width = span_kv.shape
        self.dim = width // 2
        self.piece = 2 * self.dim
        self.join = request_spans.shape[1]
        self.fresh = recomp_pos.shape[2]
        self.requests, self.rows, query_width = new_q.shape
        self.heads = query_width // self.dim
        self.recomputed = self.join * self.fresh
        self.decode = self.rows - self.recomputed
        self.block = self.heads * self.fresh
        self.tail = self.heads * self.decode
        self.height = self.join * self.block + self.tail
        self.slots = groups * self.per_group
        self.order = [0]
        for hops in range(1, groups // 2 + 1):
            self.order += [hops, groups - hops] if groups - hops > hops else [hops]

    def source(self, distance):
        return distance - 1 if distance <= self.groups // 2 else (distance + 1) % self.groups

    def way(self, distance):
        return -KV_HEADS if distance <= self.groups // 2 else KV_HEADS

    def rank(self, distance):
        near = jnp.where(distance > 0, 2 * distance - 1, 0)
        return jnp.where(distance <= self.groups // 2, near, 2 * (self.groups - distance))


def pack_kernel(plan, spans, *outs):
    dim, piece = plan.dim, plan.piece
    for s in range(plan.per_group):
        for first in range(0, plan.length, piece):
            keys = spans[s, first : first + piece, :dim].astype(jnp.float32)
            outs[s][first : first + dim, :] = keys.T.astype(jnp.bfloat16)
            outs[s][first + dim : first + piece, :dim] = spans[s, first : first + dim, dim:]
            outs[s][first + dim : first + piece, dim:] = spans[s, first + dim : first + piece, dim:]


def plan_work(plan, me, home, spans, work):
    stride = plan.requests + 1
    for chunk in range(plan.slots):
        for i in range(stride):
            work[chunk * stride + i] = 0
    for u in range(plan.requests):
        for j in range(plan.join):
            slot = home[spans[j, me[0] * plan.requests + u]]
            group = lax.div(slot, plan.per_group)
            distance = lax.rem(group - me[0] + plan.groups, plan.groups)
            chunk = plan.rank(distance) * plan.per_group + slot - group * plan.per_group
            count = work[chunk * stride] + 1
            work[chunk * stride] = count
            work[chunk * stride + count] = u * plan.join + j
            work[plan.slots * stride + u * plan.join + j] = chunk


def prepare_kernel(plan, me, home_hbm, spans_hbm, newq_hbm, newkv_hbm, recomp_hbm, q_out, acc, places, turns, marks,
                   fresh_k, fresh_v, last_kv, work, home, spans, newq, newkv, recomp, table, flat, tails, column, mask, sems):
    loads = [
        pltpu.make_async_copy(source, target, sems.at[i])
        for i, (source, target) in enumerate(
            [(home_hbm, home), (spans_hbm, spans), (recomp_hbm, recomp), (newq_hbm, newq), (newkv_hbm, newkv)]
        )
    ]
    for load in loads:
        load.start()
    dim, fresh, requests, heads, block = plan.dim, plan.fresh, plan.requests, plan.heads, plan.block
    recomputed, decode, join = plan.recomputed, plan.decode, plan.join
    half = dim // 2
    scale = LOG2E / (dim**0.5)

    row = lax.broadcasted_iota(jnp.int32, (dim, dim), 0)
    rate = turns_per_step(lax.rem(row, half), dim)
    phase = jnp.where(row < half, 0.25, 0.0)
    for j in range(join):
        turns[j] = sine_of_turns(rate * float(j * plan.length) + phase)

    number = lax.broadcasted_iota(jnp.int32, (fresh, dim), 0)
    lane = lax.broadcasted_iota(jnp.int32, (fresh, dim), 1)
    stale = (lane >= fresh) & (lane < 2 * fresh)
    own = jnp.where(stale | (lane == number), 1.0, 0.0).astype(jnp.bfloat16)
    other = jnp.where(stale, 1.0, 0.0).astype(jnp.bfloat16)
    for head in range(heads):
        marks[head * fresh : (head + 1) * fresh, :] = own
    for first in range(block, plan.height - plan.tail, fresh):
        marks[first : first + fresh, :] = other
    marks[plan.height - plan.tail :, :] = other[: plan.tail]

    number = lax.broadcasted_iota(jnp.int32, (fresh, recomputed), 0)
    key = lax.broadcasted_iota(jnp.int32, (fresh, recomputed), 1)
    for j in range(join):
        seen = jnp.where(key <= j * fresh + number, 0.0, -BIG)
        for head in range(heads):
            mask[j * block + head * fresh : j * block + (head + 1) * fresh, :] = seen
    mask[join * block :, :] = jnp.zeros((plan.tail, recomputed), jnp.float32)

    lane = lax.broadcasted_iota(jnp.int32, (fresh, dim), 1)
    rate = turns_per_step(lax.rem(lane, half), dim)
    signed = jnp.where(lane < half, -rate, rate)

    def places_of(u, carry):
        request = me[0] * requests + u
        column[:join, :fresh] = recomp[request].astype(jnp.float32)
        upright = column[...].T
        for j in range(join):
            inside = jnp.broadcast_to(upright[:fresh, j : j + 1], (fresh, dim))
            places[u * join + j] = inside
            at = inside + float(j * plan.length)
            table[0, u, j * fresh : (j + 1) * fresh, :] = sine_of_turns(at * rate + 0.25)
            table[1, u, j * fresh : (j + 1) * fresh, :] = sine_of_turns(at * signed)
        return carry

    for load in loads[:3]:
        load.wait()
    plan_work(plan, me, home, spans, work)
    column[...] = jnp.zeros(column.shape, jnp.float32)
    lax.fori_loop(0, requests, places_of, 0)
    step = lax.broadcasted_iota(jnp.int32, (decode * requests, dim), 0) // requests
    at = (join * plan.length + step).astype(jnp.float32)
    lane = lax.broadcasted_iota(jnp.int32, (decode * requests, dim), 1)
    rate = turns_per_step(lax.rem(lane, half), dim)
    last_cos = sine_of_turns(at * rate + 0.25)
    last_sin = sine_of_turns(at * jnp.where(lane < half, -rate, rate))

    for load in loads[3:]:
        load.wait()

    def queries_of(j, carry):
        rows = pl.ds(pl.multiple_of(j * fresh, fresh), fresh)
        for head in range(heads):
            x = newq[rows, :, head * dim : (head + 1) * dim].astype(jnp.float32)
            flat[head, : fresh * requests, :] = x.reshape(fresh * requests, dim)
        for u in range(requests):
            cosines = table[0, u, rows, :] * scale
            sines = table[1, u, rows, :] * scale
            for head in range(heads):
                y = turn(flat[head, pl.ds(u, fresh, stride=requests), :], cosines, sines)
                q_out[u, pl.ds(pl.multiple_of(j * block + head * fresh, fresh), fresh), :] = y.astype(jnp.bfloat16)
        return carry

    lax.fori_loop(0, join, queries_of, 0)
    for head in range(heads):
        x = newq[recomputed:, :, head * dim : (head + 1) * dim].astype(jnp.float32)
        y = turn(x.reshape(decode * requests, dim), last_cos, last_sin) * scale
        tails[head * decode * requests : (head + 1) * decode * requests, :] = y
    for u in range(requests):
        y = tails[pl.ds(u, plan.tail, stride=requests), :]
        q_out[u, join * block :, :] = y.astype(jnp.bfloat16)

    x = newkv[:recomputed, :, :].astype(jnp.float32)
    for side in range(2):
        flat[side] = x[:, :, side * dim : (side + 1) * dim].reshape(recomputed * requests, dim)
    x = newkv[recomputed:, :, :].astype(jnp.float32)
    last_kv[:, :dim] = turn(x[:, :, :dim].reshape(decode * requests, dim), last_cos, last_sin).astype(
        jnp.bfloat16
    ).astype(jnp.float32)
    last_kv[:, dim:] = x[:, :, dim:].reshape(decode * requests, dim)
    which = lax.rem(lax.broadcasted_iota(jnp.int32, (plan.tail, dim), 0), decode)
    lead = lax.broadcasted_iota(jnp.int32, (plan.tail, dim), 1) == 0

    def fresh_of(u, carry):
        y = turn(flat[0, pl.ds(u, recomputed, stride=requests), :], table[0, u], table[1, u])
        fresh_k[u] = y.T.astype(jnp.bfloat16)
        fresh_v[u] = flat[1, pl.ds(u, recomputed, stride=requests), :].astype(jnp.bfloat16)
        s = jnp.dot(q_out[u], fresh_k[u], preferred_element_type=jnp.float32)
        p = jnp.exp2(s + mask[...])
        acc[u, :, dim:] = p
        acc[u, :, :dim] = jnp.dot(p.astype(jnp.bfloat16), fresh_v[u], preferred_element_type=jnp.float32)
        mine = q_out[u, join * block :, :].astype(jnp.float32)
        for d in range(decode):
            pair = last_kv[pl.ds(d * requests + u, 1), :]
            s = jnp.sum(mine * pair[:, :dim], 1, keepdims=True)
            p = jnp.where(which >= d, jnp.exp2(jnp.broadcast_to(s, which.shape)), 0.0)
            acc[u, join * block :, :dim] += p * pair[:, dim:]
            acc[u, join * block :, dim:] += jnp.where(lead, p, 0.0)
        return carry

    for u in range(requests):
        fresh_of(u, 0)


def spread_chunk(plan, chunk, values):
    dim, piece = plan.dim, plan.piece
    for first in range(0, chunk.shape[0], piece):
        values[first : first + dim, :] = chunk[first + dim : first + piece, :dim]
        values[first + dim : first + piece, :] = chunk[first + dim : first + piece, dim:]


def shift_keys(plan, chunk, first_token, place, angles, keys):
    dim, piece, fresh = plan.dim, plan.piece, plan.fresh
    half = dim // 2
    wide = lambda x: jnp.concatenate([x] * (piece // dim), 1)
    cosines, sines = wide(angles[:half]), wide(angles[half:])
    place = wide(place)
    for first in range(0, chunk.shape[0], piece):
        columns = slice(first, first + piece)
        a = chunk[first : first + half, :].astype(jnp.float32)
        b = chunk[first + half : first + dim, :].astype(jnp.float32)
        keys[:half, columns] = (a * cosines - b * sines).astype(jnp.bfloat16)
        keys[half:dim, columns] = (b * cosines + a * sines).astype(jnp.bfloat16)
        token = lax.broadcasted_iota(jnp.int32, (fresh, piece), 1) + (first_token + first)
        token = token.astype(jnp.float32)
        keys[dim : dim + fresh, columns] = jnp.where(token > place, -BIG, 0.0).astype(jnp.bfloat16)
        keys[dim + fresh : dim + 2 * fresh, columns] = jnp.where(token == place, -BIG, 0.0).astype(jnp.bfloat16)


def chunk_kernel(plan, order, _work, chunk, places, turns, marks, q, _acc, acc, work, keys, values):
    dim, block, join = plan.dim, plan.block, plan.join
    length = chunk.shape[0]
    keys[dim + 2 * plan.fresh :, :] = jnp.zeros((dim - 2 * plan.fresh, length), jnp.bfloat16)
    spread_chunk(plan, chunk, values)
    base = order * (plan.requests + 1)

    def prepare(n):
        place = work[base + 1 + n]
        shift_keys(plan, chunk, 0, places[place], turns[lax.rem(place, join)], keys)

    def one(n, carry):
        place = work[base + 1 + n]
        u = lax.div(place, join)
        j = place - u * join
        for k in range(join):

            @pl.when(j == k)
            def _():
                count = plan.height - k * block
                left = jnp.concatenate([q[u, k * block :, :], marks[:count, :]], 1)
                s = jnp.dot(left, keys[...], preferred_element_type=jnp.float32)
                prepare(jnp.minimum(n + 1, plan.requests - 1))
                p = jnp.exp2(s)
                parts = [p[:, first : first + dim] for first in range(0, length, dim)]
                while len(parts) > 1:
                    parts = [sum(parts[i : i + 2]) for i in range(0, len(parts), 2)]
                acc[u, k * block :, dim:] += parts[0]
                acc[u, k * block :, :dim] += jnp.dot(
                    p.astype(jnp.bfloat16), values[...], preferred_element_type=jnp.float32
                )

        return carry

    prepare(0)
    lax.fori_loop(0, work[base], one, 0)


def finish_kernel(plan, work, *refs):
    chunks = refs[: plan.slots]
    (places, turns, marks, q, acc, fresh_k, fresh_v, last_kv, out,
     done, flat, tails, joined, keys, values, top, total, peak, sems, load) = refs[plan.slots :]
    dim, fresh, requests, heads, block = plan.dim, plan.fresh, plan.requests, plan.heads, plan.block
    recomputed, decode, join = plan.recomputed, plan.decode, plan.join

    def quotient(a, weight):
        inverse = pl.reciprocal(weight, approx=True)
        return a * (inverse * (2.0 - weight * inverse))

    def put(u, j, source, seen):
        after = []
        for head in range(heads):
            rows = slice(head * fresh, (head + 1) * fresh)
            a, weight = source(rows)
            o = quotient(a, weight)
            flat[j, head, pl.ds(u, fresh, stride=requests), :] = o
            least, most, every = seen[head]
            after.append((jnp.minimum(least, weight), jnp.maximum(most, weight), every + o))
        return after

    def put_tail(u, a, weight):
        o = quotient(a, weight)
        tails[pl.ds(u, plan.tail, stride=requests), :] = o
        return weight, weight, o

    def summed(u, start, count):
        a = acc[u, start : start + count, :]
        return a[:, :dim], jnp.sum(a[:, dim:], 1, keepdims=True)

    def write(j):
        rows = pl.ds(j * fresh, fresh)
        for head in range(heads):
            x = flat[j, head].reshape(fresh, requests, dim)
            done[rows, :, head * dim : (head + 1) * dim] = x.astype(jnp.bfloat16)
        return rows

    def write_tail():
        for head in range(heads):
            x = tails[head * decode * requests : (head + 1) * decode * requests, :]
            done[recomputed:, :, head * dim : (head + 1) * dim] = x.reshape(decode, requests, dim).astype(jnp.bfloat16)

    def send(j):
        rows = pl.ds(j * fresh, fresh) if j < join else pl.ds(recomputed, decode)
        return pltpu.make_async_copy(done.at[rows], out.at[rows], sems.at[j])

    def fits(seen):
        least, most, every = functools.reduce(
            lambda x, y: (jnp.minimum(x[0], y[0]), jnp.maximum(x[1], y[1]), x[2] + y[2]), seen
        )
        good = jnp.where((least > 2.0**-60) & (most < 2.0**60) & (every - every == 0.0), 1.0, 0.0)
        return jnp.min(good) > 0.5

    one, none = jnp.ones((fresh, 1), jnp.float32), jnp.zeros((fresh, dim), jnp.float32)
    clean = [(one, one, none)] * heads
    ends = [put_tail(u, *summed(u, join * block, plan.tail)) for u in range(requests)]
    write_tail()
    send(join).start()
    seen = clean
    for j in range(join):
        for u in range(requests):
            source = lambda rows: summed(u, j * block + rows.start, fresh)
            seen = put(u, j, source, seen)
        write(j)
        send(j).start()
    good = fits(ends) & fits(seen)
    for j in range(join + 1):
        send(j).wait()

    @pl.when(jnp.logical_not(good))
    def _():
        keys[dim + 2 * fresh :, :] = jnp.zeros((dim - 2 * fresh, plan.length), jnp.bfloat16)

        def fold(rows, s, v):
            before = peak[rows, :]
            now = jnp.maximum(before, jnp.max(s, 1, keepdims=True))
            peak[rows, :] = now
            fade = jnp.exp2(before - now)
            p = jnp.exp2(s - now[:, :1]).astype(jnp.bfloat16)
            total[rows, :] = total[rows, :] * fade + jnp.sum(p.astype(jnp.float32), 1, keepdims=True)
            top[rows, :] = top[rows, :] * fade + jnp.dot(p, v, preferred_element_type=jnp.float32)

        def sums(u, j):
            count = block if j < join else plan.tail
            every = pl.ds(0, count)
            peak[every, :] = jnp.full((count, dim), -3.0e38, jnp.float32)
            top[every, :] = jnp.zeros((count, dim), jnp.float32)
            total[every, :] = jnp.zeros((count, dim), jnp.float32)
            mine = q[u, j * block : j * block + count, :]
            s = jnp.dot(mine, fresh_k[u], preferred_element_type=jnp.float32)
            key = lax.broadcasted_iota(jnp.int32, s.shape, 1)
            row = lax.broadcasted_iota(jnp.int32, s.shape, 0)
            if j < join:
                s = jnp.where(key <= j * fresh + lax.rem(row, fresh), s, -BIG)
            fold(every, s, fresh_v[u])
            for k in range(min(j + 1, join)):
                for order, chunk in enumerate(chunks):

                    @pl.when(work[plan.slots * (requests + 1) + u * join + k] == order)
                    def _():
                        copy = pltpu.make_async_copy(chunk, joined, load.at[0])
                        copy.start()
                        copy.wait()

                spread_chunk(plan, joined, values)
                shift_keys(plan, joined, 0, places[u * join + k], turns[k], keys)
                mark = marks[:count, :] if k == j else marks[block : block + count, :]
                left = jnp.concatenate([mine, mark], 1)
                s = jnp.dot(left, keys[...], preferred_element_type=jnp.float32)
                fold(every, s, values[...])
            if j == join:
                which = lax.rem(lax.broadcasted_iota(jnp.int32, (count, dim), 0), decode)
                for d in range(decode):
                    pair = last_kv[pl.ds(d * requests + u, 1), :]
                    s = jnp.sum(mine.astype(jnp.float32) * pair[:, :dim], 1, keepdims=True)
                    s = jnp.where(which >= d, s, -BIG)
                    before = peak[every, :]
                    now = jnp.maximum(before, s)
                    peak[every, :] = now
                    p = jnp.exp2(s - now)
                    total[every, :] = total[every, :] * jnp.exp2(before - now) + p
                    top[every, :] = top[every, :] * jnp.exp2(before - now) + p * pair[:, dim:]

        for j in range(join + 1):

            def again(u, carry):
                sums(u, j)
                if j < join:
                    put(u, j, lambda rows: (top[rows, :], total[rows, :1]), clean)
                else:
                    put_tail(u, top[: plan.tail, :], total[: plan.tail, :1])
                return carry

            lax.fori_loop(0, requests, again, 0)
            if j < join:
                write(j)
            else:
                write_tail()
            copy = send(j)
            copy.start()
            copy.wait()


def local(span_kv, span_home, request_spans, recomp_pos, new_q, new_kv):
    groups = lax.axis_size("store") // KV_HEADS
    me = (lax.axis_index("store") // KV_HEADS).reshape(1).astype(jnp.int32)
    plan = Plan(span_kv, request_spans, recomp_pos, new_q, groups)
    dim, join, requests = plan.dim, plan.join, plan.requests
    vmem = pl.BlockSpec(memory_space=pltpu.VMEM)
    smem = pl.BlockSpec(memory_space=pltpu.SMEM)
    anywhere = pl.BlockSpec(memory_space=pl.ANY)
    params = lambda mib: pltpu.CompilerParams(vmem_limit_bytes=mib * MIB)
    inside = lambda x: pltpu.with_memory_space_constraint(x, pltpu.VMEM)
    outside = lambda x: pltpu.with_memory_space_constraint(x, pltpu.HBM)
    cost = lambda us: pl.CostEstimate(flops=int(us * 2e7), bytes_accessed=0, transcendentals=0)

    packed = pl.pallas_call(
        functools.partial(pack_kernel, plan),
        out_shape=[pltpu.VMEM((plan.length, 2 * dim), jnp.bfloat16)] * plan.per_group,
        in_specs=[vmem],
        out_specs=[vmem] * plan.per_group,
        compiler_params=params(6),
        cost_estimate=cost(1.0),
        name="pack",
    )(span_kv)

    buffers = {(0, c): x for c, x in enumerate(packed)}

    for after in plan.order[1:3]:
        for c in range(plan.per_group):
            buffers[after, c] = shifted(packed[c], "store", plan.way(after))

    spans = request_spans.T

    work_type = pltpu.SMEM((plan.slots * (requests + 1) + requests * join,), jnp.int32)
    acc_type = pltpu.VMEM((requests, plan.height, 2 * dim), jnp.float32)
    q, acc, places, turns, marks, fresh_k, fresh_v, last_kv, work = pl.pallas_call(
        functools.partial(prepare_kernel, plan),
        out_shape=[
            pltpu.VMEM((requests, plan.height, dim), jnp.bfloat16),
            acc_type,
            pltpu.VMEM((requests * join, plan.fresh, dim), jnp.float32),
            pltpu.VMEM((join, dim, dim), jnp.float32),
            pltpu.VMEM((plan.height, dim), jnp.bfloat16),
            pltpu.VMEM((requests, dim, plan.recomputed), jnp.bfloat16),
            pltpu.VMEM((requests, plan.recomputed, dim), jnp.bfloat16),
            pltpu.VMEM((plan.decode * requests, 2 * dim), jnp.float32),
            work_type,
        ],
        in_specs=[smem] + [anywhere] * 5,
        out_specs=[vmem] * 8 + [smem],
        scratch_shapes=[
            pltpu.SMEM(span_home.shape, jnp.int32),
            pltpu.SMEM(spans.shape, jnp.int32),
            pltpu.VMEM((plan.rows, requests, new_q.shape[2]), jnp.bfloat16),
            pltpu.VMEM((plan.rows, requests, 2 * dim), jnp.bfloat16),
            pltpu.VMEM(recomp_pos.shape, jnp.int32),
            pltpu.VMEM((2, requests, plan.recomputed, dim), jnp.float32),
            pltpu.VMEM((plan.heads, plan.recomputed * requests, dim), jnp.float32),
            pltpu.VMEM((plan.heads * plan.decode * requests, dim), jnp.float32),
            pltpu.VMEM((dim, dim), jnp.float32),
            pltpu.VMEM((plan.height, plan.recomputed), jnp.float32),
            pltpu.SemaphoreType.DMA((5,)),
        ],
        compiler_params=params(20),
        cost_estimate=cost(6.0),
        name="prepare",
    )(me, *map(outside, [span_home, spans, new_q.transpose(1, 0, 2), new_kv.transpose(1, 0, 2), recomp_pos]))
    scalar = lambda x: pltpu.with_memory_space_constraint(x, pltpu.SMEM)

    def take(order, chunk, acc, work):
        return pl.pallas_call(
            functools.partial(chunk_kernel, plan, order),
            out_shape=[acc_type, work_type],
            in_specs=[smem] + [vmem] * 6,
            out_specs=[vmem, smem],
            input_output_aliases={6: 0, 0: 1},
            scratch_shapes=[
                pltpu.VMEM((2 * dim, plan.length), jnp.bfloat16),
                pltpu.VMEM((plan.length, dim), jnp.bfloat16),
            ],
            compiler_params=params(12),
            cost_estimate=cost(2.5),
            name="chunk",
        )(scalar(work), *map(inside, [chunk, places, turns, marks, q, acc]))

    def onward(distance, c, work):
        for after in plan.order:
            if distance > 0 and after > 0 and plan.source(after) == distance:
                buffers[distance, c], work = lax.optimization_barrier((buffers[distance, c], work))
                buffers[after, c] = shifted(buffers[distance, c], "store", plan.way(after))
        return work

    chunks = [(distance, c) for distance in plan.order for c in range(plan.per_group)]
    first = plan.per_group
    if groups > 1:
        work = onward(*chunks[first], work)
    for order, (distance, c) in enumerate(chunks):
        acc, work = take(order, buffers[distance, c], acc, work)
        if order > first:
            work = onward(distance, c, work)
    buffers = [buffers[chunk] for chunk in chunks]

    out = pl.pallas_call(
        functools.partial(finish_kernel, plan),
        out_shape=jax.ShapeDtypeStruct((plan.rows, requests, new_q.shape[2]), jnp.bfloat16),
        in_specs=[smem] + [anywhere] * len(buffers) + [vmem] * 8,
        out_specs=anywhere,
        scratch_shapes=[
            pltpu.VMEM((plan.rows, requests, new_q.shape[2]), jnp.bfloat16),
            pltpu.VMEM((join, plan.heads, plan.fresh * requests, dim), jnp.float32),
            pltpu.VMEM((plan.heads * plan.decode * requests, dim), jnp.float32),
            pltpu.VMEM((plan.length, 2 * dim), jnp.bfloat16),
            pltpu.VMEM((2 * dim, plan.length), jnp.bfloat16),
            pltpu.VMEM((plan.length, dim), jnp.bfloat16),
            pltpu.VMEM((plan.block, dim), jnp.float32),
            pltpu.VMEM((plan.block, dim), jnp.float32),
            pltpu.VMEM((plan.block, dim), jnp.float32),
            pltpu.SemaphoreType.DMA((join + 1,)),
            pltpu.SemaphoreType.DMA((1,)),
        ],
        compiler_params=params(24),
        cost_estimate=cost(3.0),
        name="finish",
    )(scalar(work), *buffers, *map(inside, [places, turns, marks, q, acc, fresh_k, fresh_v, last_kv]))
    return out.transpose(1, 0, 2)


def solution(mesh):
    return jax.shard_map(
        local,
        mesh=mesh,
        in_specs=(
            P(("groups", "store"), None, None),
            P("groups"),
            P("groups", None),
            P("groups", None, None),
            P(("groups", "store"), None, None),
            P(("groups", "store"), None, None),
        ),
        out_specs=P(("groups", "store"), None, None),
        check_vma=False,
    )
```

```python
import functools
import math

import jax
import jax.numpy as jnp
from jax import lax
from jax.experimental import pallas as pl
from jax.experimental.pallas import tpu as pltpu
from jax.sharding import PartitionSpec as P

KV_HEADS = 8
LOG2E = 1.4426950408889634
BIG = 2.0**100
MIB = 1 << 20
SINE = (6.283185272447939, -41.34169703819957, 81.60502363802357, -76.7015376701132,
        42.01607576102491, -14.868322748754837, 3.1993388405088488)


def shifted(value, axis, by):
    devices = lax.axis_size(axis)
    return lax.ppermute(value, axis, [(i, (i + by) % devices) for i in range(devices)])


def sine_of_turns(t):
    r = t - jnp.floor(t + 0.5)
    square = r * r
    value = jnp.full(r.shape, SINE[-1], jnp.float32)
    for coefficient in SINE[-2::-1]:
        value = value * square + coefficient
    return value * r


def turns_per_step(index, dim):
    return jnp.exp(-(2.0 / dim) * math.log(500000.0) * index.astype(jnp.float32)) * (0.5 / math.pi)


def turn(rows, cosines, sines):
    return rows * cosines + pltpu.roll(rows, rows.shape[-1] // 2, 1) * sines


class Plan:
    def __init__(self, span_kv, request_spans, recomp_pos, new_q, groups):
        self.groups = groups
        self.per_group, self.length, width = span_kv.shape
        self.dim = width // 2
        self.piece = 2 * self.dim
        self.join = request_spans.shape[1]
        self.fresh = recomp_pos.shape[2]
        self.requests, self.rows, query_width = new_q.shape
        self.heads = query_width // self.dim
        self.recomputed = self.join * self.fresh
        self.decode = self.rows - self.recomputed
        self.block = self.heads * self.fresh
        self.tail = self.heads * self.decode
        self.height = self.join * self.block + self.tail
        self.slots = groups * self.per_group
        self.order = [0]
        for hops in range(1, groups // 2 + 1):
            self.order += [hops, groups - hops] if groups - hops > hops else [hops]

    def source(self, distance):
        return distance - 1 if distance <= self.groups // 2 else (distance + 1) % self.groups

    def way(self, distance):
        return -KV_HEADS if distance <= self.groups // 2 else KV_HEADS

    def rank(self, distance):
        near = jnp.where(distance > 0, 2 * distance - 1, 0)
        return jnp.where(distance <= self.groups // 2, near, 2 * (self.groups - distance))


def pack_kernel(plan, spans, *outs):
    dim, piece = plan.dim, plan.piece
    for s in range(plan.per_group):
        for first in range(0, plan.length, piece):
            keys = spans[s, first : first + piece, :dim].astype(jnp.float32)
            outs[s][first : first + dim, :] = keys.T.astype(jnp.bfloat16)
            outs[s][first + dim : first + piece, :dim] = spans[s, first : first + dim, dim:]
            outs[s][first + dim : first + piece, dim:] = spans[s, first + dim : first + piece, dim:]


def plan_work(plan, me, home, spans, work):
    stride = plan.requests + 1
    for chunk in range(plan.slots):
        for i in range(stride):
            work[chunk * stride + i] = 0
    for u in range(plan.requests):
        for j in range(plan.join):
            slot = home[spans[j, me[0] * plan.requests + u]]
            group = lax.div(slot, plan.per_group)
            distance = lax.rem(group - me[0] + plan.groups, plan.groups)
            chunk = plan.rank(distance) * plan.per_group + slot - group * plan.per_group
            count = work[chunk * stride] + 1
            work[chunk * stride] = count
            work[chunk * stride + count] = u * plan.join + j
            work[plan.slots * stride + u * plan.join + j] = chunk


def prepare_kernel(plan, me, home_hbm, spans_hbm, newq_hbm, newkv_hbm, recomp_hbm, q_out, acc, places, turns, marks,
                   fresh_k, fresh_v, last_kv, work, home, spans, newq, newkv, recomp, table, flat, tails, column, mask, sems):
    loads = [
        pltpu.make_async_copy(source, target, sems.at[i])
        for i, (source, target) in enumerate(
            [(home_hbm, home), (spans_hbm, spans), (recomp_hbm, recomp), (newq_hbm, newq), (newkv_hbm, newkv)]
        )
    ]
    for load in loads:
        load.start()
    dim, fresh, requests, heads, block = plan.dim, plan.fresh, plan.requests, plan.heads, plan.block
    recomputed, decode, join = plan.recomputed, plan.decode, plan.join
    half = dim // 2
    scale = LOG2E / (dim**0.5)

    row = lax.broadcasted_iota(jnp.int32, (dim, dim), 0)
    rate = turns_per_step(lax.rem(row, half), dim)
    phase = jnp.where(row < half, 0.25, 0.0)
    for j in range(join):
        turns[j] = sine_of_turns(rate * float(j * plan.length) + phase)

    number = lax.broadcasted_iota(jnp.int32, (fresh, dim), 0)
    lane = lax.broadcasted_iota(jnp.int32, (fresh, dim), 1)
    stale = (lane >= fresh) & (lane < 2 * fresh)
    own = jnp.where(stale | (lane == number), 1.0, 0.0).astype(jnp.bfloat16)
    other = jnp.where(stale, 1.0, 0.0).astype(jnp.bfloat16)
    for head in range(heads):
        marks[head * fresh : (head + 1) * fresh, :] = own
    for first in range(block, plan.height - plan.tail, fresh):
        marks[first : first + fresh, :] = other
    marks[plan.height - plan.tail :, :] = other[: plan.tail]

    number = lax.broadcasted_iota(jnp.int32, (fresh, recomputed), 0)
    key = lax.broadcasted_iota(jnp.int32, (fresh, recomputed), 1)
    for j in range(join):
        seen = jnp.where(key <= j * fresh + number, 0.0, -BIG)
        for head in range(heads):
            mask[j * block + head * fresh : j * block + (head + 1) * fresh, :] = seen
    mask[join * block :, :] = jnp.zeros((plan.tail, recomputed), jnp.float32)

    lane = lax.broadcasted_iota(jnp.int32, (fresh, dim), 1)
    rate = turns_per_step(lax.rem(lane, half), dim)
    signed = jnp.where(lane < half, -rate, rate)

    def places_of(u):
        request = me[0] * requests + u
        column[:join, :fresh] = recomp[request].astype(jnp.float32)
        upright = column[...].T
        for j in range(join):
            inside = jnp.broadcast_to(upright[:fresh, j : j + 1], (fresh, dim))
            places[u * join + j] = inside
            at = inside + float(j * plan.length)
            table[0, u, j * fresh : (j + 1) * fresh, :] = sine_of_turns(at * rate + 0.25)
            table[1, u, j * fresh : (j + 1) * fresh, :] = sine_of_turns(at * signed)

    for load in loads[:3]:
        load.wait()
    plan_work(plan, me, home, spans, work)
    column[...] = jnp.zeros(column.shape, jnp.float32)
    for u in range(requests):
        places_of(u)
    step = lax.broadcasted_iota(jnp.int32, (decode * requests, dim), 0) // requests
    at = (join * plan.length + step).astype(jnp.float32)
    lane = lax.broadcasted_iota(jnp.int32, (decode * requests, dim), 1)
    rate = turns_per_step(lax.rem(lane, half), dim)
    last_cos = sine_of_turns(at * rate + 0.25)
    last_sin = sine_of_turns(at * jnp.where(lane < half, -rate, rate))

    for load in loads[3:]:
        load.wait()

    def queries_of(j):
        rows = slice(j * fresh, (j + 1) * fresh)
        for head in range(heads):
            x = newq[rows, :, head * dim : (head + 1) * dim].astype(jnp.float32)
            flat[head, : fresh * requests, :] = x.reshape(fresh * requests, dim)
        for u in range(requests):
            cosines = table[0, u, rows, :] * scale
            sines = table[1, u, rows, :] * scale
            for head in range(heads):
                y = turn(flat[head, pl.ds(u, fresh, stride=requests), :], cosines, sines)
                q_out[u, pl.ds(j * block + head * fresh, fresh), :] = y.astype(jnp.bfloat16)

    for j in range(join):
        queries_of(j)
    for head in range(heads):
        x = newq[recomputed:, :, head * dim : (head + 1) * dim].astype(jnp.float32)
        y = turn(x.reshape(decode * requests, dim), last_cos, last_sin) * scale
        tails[head * decode * requests : (head + 1) * decode * requests, :] = y
    for u in range(requests):
        y = tails[pl.ds(u, plan.tail, stride=requests), :]
        q_out[u, join * block :, :] = y.astype(jnp.bfloat16)

    x = newkv[:recomputed, :, :].astype(jnp.float32)
    for side in range(2):
        flat[side] = x[:, :, side * dim : (side + 1) * dim].reshape(recomputed * requests, dim)
    x = newkv[recomputed:, :, :].astype(jnp.float32)
    last_kv[:, :dim] = turn(x[:, :, :dim].reshape(decode * requests, dim), last_cos, last_sin).astype(
        jnp.bfloat16
    ).astype(jnp.float32)
    last_kv[:, dim:] = x[:, :, dim:].reshape(decode * requests, dim)
    which = lax.rem(lax.broadcasted_iota(jnp.int32, (plan.tail, dim), 0), decode)
    lead = lax.broadcasted_iota(jnp.int32, (plan.tail, dim), 1) == 0

    def fresh_of(u):
        y = turn(flat[0, pl.ds(u, recomputed, stride=requests), :], table[0, u], table[1, u])
        fresh_k[u] = y.T.astype(jnp.bfloat16)
        fresh_v[u] = flat[1, pl.ds(u, recomputed, stride=requests), :].astype(jnp.bfloat16)
        s = jnp.dot(q_out[u], fresh_k[u], preferred_element_type=jnp.float32)
        p = jnp.exp2(s + mask[...])
        acc[u, :, dim:] = p
        acc[u, :, :dim] = jnp.dot(p.astype(jnp.bfloat16), fresh_v[u], preferred_element_type=jnp.float32)
        mine = q_out[u, join * block :, :].astype(jnp.float32)
        for d in range(decode):
            pair = last_kv[pl.ds(d * requests + u, 1), :]
            s = jnp.sum(mine * pair[:, :dim], 1, keepdims=True)
            p = jnp.where(which >= d, jnp.exp2(jnp.broadcast_to(s, which.shape)), 0.0)
            acc[u, join * block :, :dim] += p * pair[:, dim:]
            acc[u, join * block :, dim:] += jnp.where(lead, p, 0.0)

    for u in range(requests):
        fresh_of(u)


def spread_chunk(plan, chunk, values):
    dim, piece = plan.dim, plan.piece
    for first in range(0, chunk.shape[0], piece):
        values[first : first + dim, :] = chunk[first + dim : first + piece, :dim]
        values[first + dim : first + piece, :] = chunk[first + dim : first + piece, dim:]


def shift_keys(plan, chunk, first_token, place, angles, keys):
    dim, piece, fresh = plan.dim, plan.piece, plan.fresh
    half = dim // 2
    wide = lambda x: jnp.concatenate([x] * (piece // dim), 1)
    cosines, sines = wide(angles[:half]), wide(angles[half:])
    place = wide(place)
    for first in range(0, chunk.shape[0], piece):
        columns = slice(first, first + piece)
        a = chunk[first : first + half, :].astype(jnp.float32)
        b = chunk[first + half : first + dim, :].astype(jnp.float32)
        keys[:half, columns] = (a * cosines - b * sines).astype(jnp.bfloat16)
        keys[half:dim, columns] = (b * cosines + a * sines).astype(jnp.bfloat16)
        token = lax.broadcasted_iota(jnp.int32, (fresh, piece), 1) + (first_token + first)
        token = token.astype(jnp.float32)
        keys[dim : dim + fresh, columns] = jnp.where(token > place, -BIG, 0.0).astype(jnp.bfloat16)
        keys[dim + fresh : dim + 2 * fresh, columns] = jnp.where(token == place, -BIG, 0.0).astype(jnp.bfloat16)


def chunk_kernel(plan, order, _work, chunk, places, turns, marks, q, _acc, acc, work, keys, values):
    dim, block, join = plan.dim, plan.block, plan.join
    length = chunk.shape[0]
    keys[dim + 2 * plan.fresh :, :] = jnp.zeros((dim - 2 * plan.fresh, length), jnp.bfloat16)
    spread_chunk(plan, chunk, values)
    base = order * (plan.requests + 1)

    def prepare(n):
        place = work[base + 1 + n]
        shift_keys(plan, chunk, 0, places[place], turns[lax.rem(place, join)], keys)

    def one(n, carry):
        place = work[base + 1 + n]
        u = lax.div(place, join)
        j = place - u * join
        for k in range(join):

            @pl.when(j == k)
            def _():
                count = plan.height - k * block
                left = jnp.concatenate([q[u, k * block :, :], marks[:count, :]], 1)
                s = jnp.dot(left, keys[...], preferred_element_type=jnp.float32)
                prepare(jnp.minimum(n + 1, plan.requests - 1))
                p = jnp.exp2(s)
                parts = [p[:, first : first + dim] for first in range(0, length, dim)]
                while len(parts) > 1:
                    parts = [sum(parts[i : i + 2]) for i in range(0, len(parts), 2)]
                acc[u, k * block :, dim:] += parts[0]
                acc[u, k * block :, :dim] += jnp.dot(
                    p.astype(jnp.bfloat16), values[...], preferred_element_type=jnp.float32
                )

        return carry

    prepare(0)
    lax.fori_loop(0, work[base], one, 0)


def finish_kernel(plan, work, *refs):
    chunks = refs[: plan.slots]
    (places, turns, marks, q, acc, fresh_k, fresh_v, last_kv, out,
     done, flat, tails, joined, keys, values, top, total, peak, sems, load) = refs[plan.slots :]
    dim, fresh, requests, heads, block = plan.dim, plan.fresh, plan.requests, plan.heads, plan.block
    recomputed, decode, join = plan.recomputed, plan.decode, plan.join

    def quotient(a, weight):
        return a * pl.reciprocal(weight, approx=True)

    def tree(join_two, items):
        while len(items) > 1:
            items = [functools.reduce(join_two, items[i : i + 2]) for i in range(0, len(items), 2)]
        return items[0]

    def put(u, j, source, seen):
        weights, quotients = [], []
        for head in range(heads):
            a, weight = source(slice(head * fresh, (head + 1) * fresh))
            o = quotient(a, weight)
            flat[j, head, pl.ds(u, fresh, stride=requests), :] = o
            weights.append(weight)
            quotients.append(o)
        least, most, every = seen
        least = jnp.minimum(least, tree(jnp.minimum, weights))
        most = jnp.maximum(most, tree(jnp.maximum, weights))
        return least, most, every + tree(jnp.add, quotients)

    def put_tail(u, a, weight):
        o = quotient(a, weight)
        tails[pl.ds(u, plan.tail, stride=requests), :] = o
        return weight, weight, o

    def summed(u, start, count):
        a = acc[u, start : start + count, :]
        return a[:, :dim], jnp.sum(a[:, dim:], 1, keepdims=True)

    def write(j):
        rows = pl.ds(j * fresh, fresh)
        for head in range(heads):
            x = flat[j, head].reshape(fresh, requests, dim)
            done[rows, :, head * dim : (head + 1) * dim] = x.astype(jnp.bfloat16)
        return rows

    def write_tail():
        for head in range(heads):
            x = tails[head * decode * requests : (head + 1) * decode * requests, :]
            done[recomputed:, :, head * dim : (head + 1) * dim] = x.reshape(decode, requests, dim).astype(jnp.bfloat16)

    def send(j):
        rows = pl.ds(j * fresh, fresh) if j < join else pl.ds(recomputed, decode)
        return pltpu.make_async_copy(done.at[rows], out.at[rows], sems.at[j])

    def fits(least, most, every):
        good = (least > 2.0**-60) & (most < 2.0**60) & (every - every == 0.0)
        return jnp.min(jnp.where(good, 1.0, 0.0)) > 0.5

    one, none = jnp.ones((fresh, 1), jnp.float32), jnp.zeros((fresh, dim), jnp.float32)
    clean = (one, one, none)
    ends = [put_tail(u, *summed(u, join * block, plan.tail)) for u in range(requests)]
    ends = [tree(*pair) for pair in zip((jnp.minimum, jnp.maximum, jnp.add), map(list, zip(*ends)))]
    write_tail()
    send(join).start()
    seen = clean
    for j in range(join):
        for u in range(requests):
            source = lambda rows: summed(u, j * block + rows.start, fresh)
            seen = put(u, j, source, seen)
        write(j)
        send(j).start()
    good = fits(*ends) & fits(*seen)
    for j in range(join + 1):
        send(j).wait()

    @pl.when(jnp.logical_not(good))
    def _():
        keys[dim + 2 * fresh :, :] = jnp.zeros((dim - 2 * fresh, plan.length), jnp.bfloat16)

        def fold(rows, s, v):
            before = peak[rows, :]
            now = jnp.maximum(before, jnp.max(s, 1, keepdims=True))
            peak[rows, :] = now
            fade = jnp.exp2(before - now)
            p = jnp.exp2(s - now[:, :1]).astype(jnp.bfloat16)
            total[rows, :] = total[rows, :] * fade + jnp.sum(p.astype(jnp.float32), 1, keepdims=True)
            top[rows, :] = top[rows, :] * fade + jnp.dot(p, v, preferred_element_type=jnp.float32)

        def sums(u, j):
            count = block if j < join else plan.tail
            every = pl.ds(0, count)
            peak[every, :] = jnp.full((count, dim), -3.0e38, jnp.float32)
            top[every, :] = jnp.zeros((count, dim), jnp.float32)
            total[every, :] = jnp.zeros((count, dim), jnp.float32)
            mine = q[u, j * block : j * block + count, :]
            s = jnp.dot(mine, fresh_k[u], preferred_element_type=jnp.float32)
            key = lax.broadcasted_iota(jnp.int32, s.shape, 1)
            row = lax.broadcasted_iota(jnp.int32, s.shape, 0)
            if j < join:
                s = jnp.where(key <= j * fresh + lax.rem(row, fresh), s, -BIG)
            fold(every, s, fresh_v[u])
            for k in range(min(j + 1, join)):
                for order, chunk in enumerate(chunks):

                    @pl.when(work[plan.slots * (requests + 1) + u * join + k] == order)
                    def _():
                        copy = pltpu.make_async_copy(chunk, joined, load.at[0])
                        copy.start()
                        copy.wait()

                spread_chunk(plan, joined, values)
                shift_keys(plan, joined, 0, places[u * join + k], turns[k], keys)
                mark = marks[:count, :] if k == j else marks[block : block + count, :]
                left = jnp.concatenate([mine, mark], 1)
                s = jnp.dot(left, keys[...], preferred_element_type=jnp.float32)
                fold(every, s, values[...])
            if j == join:
                which = lax.rem(lax.broadcasted_iota(jnp.int32, (count, dim), 0), decode)
                for d in range(decode):
                    pair = last_kv[pl.ds(d * requests + u, 1), :]
                    s = jnp.sum(mine.astype(jnp.float32) * pair[:, :dim], 1, keepdims=True)
                    s = jnp.where(which >= d, s, -BIG)
                    before = peak[every, :]
                    now = jnp.maximum(before, s)
                    peak[every, :] = now
                    p = jnp.exp2(s - now)
                    total[every, :] = total[every, :] * jnp.exp2(before - now) + p
                    top[every, :] = top[every, :] * jnp.exp2(before - now) + p * pair[:, dim:]

        for j in range(join + 1):

            def again(u, carry):
                sums(u, j)
                if j < join:
                    put(u, j, lambda rows: (top[rows, :], total[rows, :1]), clean)
                else:
                    put_tail(u, top[: plan.tail, :], total[: plan.tail, :1])
                return carry

            lax.fori_loop(0, requests, again, 0)
            if j < join:
                write(j)
            else:
                write_tail()
            copy = send(j)
            copy.start()
            copy.wait()


def local(span_kv, span_home, request_spans, recomp_pos, new_q, new_kv):
    groups = lax.axis_size("store") // KV_HEADS
    me = (lax.axis_index("store") // KV_HEADS).reshape(1).astype(jnp.int32)
    plan = Plan(span_kv, request_spans, recomp_pos, new_q, groups)
    dim, join, requests = plan.dim, plan.join, plan.requests
    vmem = pl.BlockSpec(memory_space=pltpu.VMEM)
    smem = pl.BlockSpec(memory_space=pltpu.SMEM)
    anywhere = pl.BlockSpec(memory_space=pl.ANY)
    params = lambda mib: pltpu.CompilerParams(vmem_limit_bytes=mib * MIB)
    inside = lambda x: pltpu.with_memory_space_constraint(x, pltpu.VMEM)
    outside = lambda x: pltpu.with_memory_space_constraint(x, pltpu.HBM)
    cost = lambda us: pl.CostEstimate(flops=int(us * 2e7), bytes_accessed=0, transcendentals=0)

    packed = pl.pallas_call(
        functools.partial(pack_kernel, plan),
        out_shape=[pltpu.VMEM((plan.length, 2 * dim), jnp.bfloat16)] * plan.per_group,
        in_specs=[vmem],
        out_specs=[vmem] * plan.per_group,
        compiler_params=params(6),
        cost_estimate=cost(1.0),
        name="pack",
    )(span_kv)

    buffers = {(0, c): x for c, x in enumerate(packed)}

    for after in plan.order[1:3]:
        for c in range(plan.per_group):
            buffers[after, c] = shifted(packed[c], "store", plan.way(after))

    spans = request_spans.T

    work_type = pltpu.SMEM((plan.slots * (requests + 1) + requests * join,), jnp.int32)
    acc_type = pltpu.VMEM((requests, plan.height, 2 * dim), jnp.float32)
    q, acc, places, turns, marks, fresh_k, fresh_v, last_kv, work = pl.pallas_call(
        functools.partial(prepare_kernel, plan),
        out_shape=[
            pltpu.VMEM((requests, plan.height, dim), jnp.bfloat16),
            acc_type,
            pltpu.VMEM((requests * join, plan.fresh, dim), jnp.float32),
            pltpu.VMEM((join, dim, dim), jnp.float32),
            pltpu.VMEM((plan.height, dim), jnp.bfloat16),
            pltpu.VMEM((requests, dim, plan.recomputed), jnp.bfloat16),
            pltpu.VMEM((requests, plan.recomputed, dim), jnp.bfloat16),
            pltpu.VMEM((plan.decode * requests, 2 * dim), jnp.float32),
            work_type,
        ],
        in_specs=[smem] + [anywhere] * 5,
        out_specs=[vmem] * 8 + [smem],
        scratch_shapes=[
            pltpu.SMEM(span_home.shape, jnp.int32),
            pltpu.SMEM(spans.shape, jnp.int32),
            pltpu.VMEM((plan.rows, requests, new_q.shape[2]), jnp.bfloat16),
            pltpu.VMEM((plan.rows, requests, 2 * dim), jnp.bfloat16),
            pltpu.VMEM(recomp_pos.shape, jnp.int32),
            pltpu.VMEM((2, requests, plan.recomputed, dim), jnp.float32),
            pltpu.VMEM((plan.heads, plan.recomputed * requests, dim), jnp.float32),
            pltpu.VMEM((plan.heads * plan.decode * requests, dim), jnp.float32),
            pltpu.VMEM((dim, dim), jnp.float32),
            pltpu.VMEM((plan.height, plan.recomputed), jnp.float32),
            pltpu.SemaphoreType.DMA((5,)),
        ],
        compiler_params=params(20),
        cost_estimate=cost(6.0),
        name="prepare",
    )(me, *map(outside, [span_home, spans, new_q.transpose(1, 0, 2), new_kv.transpose(1, 0, 2), recomp_pos]))
    scalar = lambda x: pltpu.with_memory_space_constraint(x, pltpu.SMEM)

    def take(order, chunk, acc, work):
        return pl.pallas_call(
            functools.partial(chunk_kernel, plan, order),
            out_shape=[acc_type, work_type],
            in_specs=[smem] + [vmem] * 6,
            out_specs=[vmem, smem],
            input_output_aliases={6: 0, 0: 1},
            scratch_shapes=[
                pltpu.VMEM((2 * dim, plan.length), jnp.bfloat16),
                pltpu.VMEM((plan.length, dim), jnp.bfloat16),
            ],
            compiler_params=params(12),
            cost_estimate=cost(2.5),
            name="chunk",
        )(scalar(work), *map(inside, [chunk, places, turns, marks, q, acc]))

    def onward(distance, c, work):
        for after in plan.order:
            if distance > 0 and after > 0 and plan.source(after) == distance:
                buffers[distance, c], work = lax.optimization_barrier((buffers[distance, c], work))
                buffers[after, c] = shifted(buffers[distance, c], "store", plan.way(after))
        return work

    chunks = [(distance, c) for distance in plan.order for c in range(plan.per_group)]
    first = plan.per_group
    if groups > 1:
        work = onward(*chunks[first], work)
    for order, (distance, c) in enumerate(chunks):
        acc, work = take(order, buffers[distance, c], acc, work)
        if order > first:
            work = onward(distance, c, work)
    buffers = [buffers[chunk] for chunk in chunks]

    out = pl.pallas_call(
        functools.partial(finish_kernel, plan),
        out_shape=jax.ShapeDtypeStruct((plan.rows, requests, new_q.shape[2]), jnp.bfloat16),
        in_specs=[smem] + [anywhere] * len(buffers) + [vmem] * 8,
        out_specs=anywhere,
        scratch_shapes=[
            pltpu.VMEM((plan.rows, requests, new_q.shape[2]), jnp.bfloat16),
            pltpu.VMEM((join, plan.heads, plan.fresh * requests, dim), jnp.float32),
            pltpu.VMEM((plan.heads * plan.decode * requests, dim), jnp.float32),
            pltpu.VMEM((plan.length, 2 * dim), jnp.bfloat16),
            pltpu.VMEM((2 * dim, plan.length), jnp.bfloat16),
            pltpu.VMEM((plan.length, dim), jnp.bfloat16),
            pltpu.VMEM((plan.block, dim), jnp.float32),
            pltpu.VMEM((plan.block, dim), jnp.float32),
            pltpu.VMEM((plan.block, dim), jnp.float32),
            pltpu.SemaphoreType.DMA((join + 1,)),
            pltpu.SemaphoreType.DMA((1,)),
        ],
        compiler_params=params(24),
        cost_estimate=cost(3.0),
        name="finish",
    )(scalar(work), *buffers, *map(inside, [places, turns, marks, q, acc, fresh_k, fresh_v, last_kv]))
    return out.transpose(1, 0, 2)


def solution(mesh):
    return jax.shard_map(
        local,
        mesh=mesh,
        in_specs=(
            P(("groups", "store"), None, None),
            P("groups"),
            P("groups", None),
            P("groups", None, None),
            P(("groups", "store"), None, None),
            P(("groups", "store"), None, None),
        ),
        out_specs=P(("groups", "store"), None, None),
        check_vma=False,
    )
```

```python
import functools
import math

import jax
import jax.numpy as jnp
from jax import lax
from jax.experimental import pallas as pl
from jax.experimental.pallas import tpu as pltpu
from jax.sharding import PartitionSpec as P

KV_HEADS = 8
LOG2E = 1.4426950408889634
BIG = 2.0**100
MIB = 1 << 20
SINE = (6.283185272447939, -41.34169703819957, 81.60502363802357, -76.7015376701132,
        42.01607576102491, -14.868322748754837, 3.1993388405088488)


def shifted(value, axis, by):
    devices = lax.axis_size(axis)
    return lax.ppermute(value, axis, [(i, (i + by) % devices) for i in range(devices)])


def sine_of_turns(t):
    r = t - jnp.floor(t + 0.5)
    square = r * r
    value = jnp.full(r.shape, SINE[-1], jnp.float32)
    for coefficient in SINE[-2::-1]:
        value = value * square + coefficient
    return value * r


def turns_per_step(index, dim):
    return jnp.exp(-(2.0 / dim) * math.log(500000.0) * index.astype(jnp.float32)) * (0.5 / math.pi)


def turn(rows, cosines, sines):
    return rows * cosines + pltpu.roll(rows, rows.shape[-1] // 2, 1) * sines


class Plan:
    def __init__(self, span_kv, request_spans, recomp_pos, new_q, groups):
        self.groups = groups
        self.per_group, self.length, width = span_kv.shape
        self.dim = width // 2
        self.piece = 2 * self.dim
        self.join = request_spans.shape[1]
        self.fresh = recomp_pos.shape[2]
        self.requests, self.rows, query_width = new_q.shape
        self.heads = query_width // self.dim
        self.recomputed = self.join * self.fresh
        self.decode = self.rows - self.recomputed
        self.block = self.heads * self.fresh
        self.tail = self.heads * self.decode
        self.height = self.join * self.block + self.tail
        self.slots = groups * self.per_group
        self.order = [0]
        for hops in range(1, groups // 2 + 1):
            self.order += [hops, groups - hops] if groups - hops > hops else [hops]

    def source(self, distance):
        return distance - 1 if distance <= self.groups // 2 else (distance + 1) % self.groups

    def way(self, distance):
        return -KV_HEADS if distance <= self.groups // 2 else KV_HEADS

    def rank(self, distance):
        near = jnp.where(distance > 0, 2 * distance - 1, 0)
        return jnp.where(distance <= self.groups // 2, near, 2 * (self.groups - distance))


def pack_kernel(plan, spans, *outs):
    dim, piece = plan.dim, plan.piece
    for s in range(plan.per_group):
        for first in range(0, plan.length, piece):
            keys = spans[s, first : first + piece, :dim].astype(jnp.float32)
            outs[s][first : first + dim, :] = keys.T.astype(jnp.bfloat16)
            outs[s][first + dim : first + piece, :dim] = spans[s, first : first + dim, dim:]
            outs[s][first + dim : first + piece, dim:] = spans[s, first + dim : first + piece, dim:]


def plan_work(plan, me, home, spans, work):
    stride = plan.requests + 1
    for chunk in range(plan.slots):
        for i in range(stride):
            work[chunk * stride + i] = 0
    for u in range(plan.requests):
        for j in range(plan.join):
            slot = home[spans[j, me[0] * plan.requests + u]]
            group = lax.div(slot, plan.per_group)
            distance = lax.rem(group - me[0] + plan.groups, plan.groups)
            chunk = plan.rank(distance) * plan.per_group + slot - group * plan.per_group
            count = work[chunk * stride] + 1
            work[chunk * stride] = count
            work[chunk * stride + count] = u * plan.join + j
            work[plan.slots * stride + u * plan.join + j] = chunk


def prepare_kernel(plan, me, home_hbm, spans_hbm, newq_hbm, newkv_hbm, recomp_hbm, q_out, acc, places, turns, marks,
                   fresh_k, fresh_v, last_kv, work, home, spans, newq, newkv, recomp, table, flat, tails, column, mask, sems):
    loads = [
        pltpu.make_async_copy(source, target, sems.at[i])
        for i, (source, target) in enumerate(
            [(home_hbm, home), (spans_hbm, spans), (recomp_hbm, recomp), (newq_hbm, newq), (newkv_hbm, newkv)]
        )
    ]
    for load in loads:
        load.start()
    dim, fresh, requests, heads, block = plan.dim, plan.fresh, plan.requests, plan.heads, plan.block
    recomputed, decode, join = plan.recomputed, plan.decode, plan.join
    half = dim // 2
    scale = LOG2E / (dim**0.5)

    row = lax.broadcasted_iota(jnp.int32, (dim, dim), 0)
    rate = turns_per_step(lax.rem(row, half), dim)
    phase = jnp.where(row < half, 0.25, 0.0)
    for j in range(join):
        turns[j] = sine_of_turns(rate * float(j * plan.length) + phase)

    number = lax.broadcasted_iota(jnp.int32, (fresh, dim), 0)
    lane = lax.broadcasted_iota(jnp.int32, (fresh, dim), 1)
    stale = (lane >= fresh) & (lane < 2 * fresh)
    own = jnp.where(stale | (lane == number), 1.0, 0.0).astype(jnp.bfloat16)
    other = jnp.where(stale, 1.0, 0.0).astype(jnp.bfloat16)
    for head in range(heads):
        marks[head * fresh : (head + 1) * fresh, :] = own
    for first in range(block, plan.height - plan.tail, fresh):
        marks[first : first + fresh, :] = other
    marks[plan.height - plan.tail :, :] = other[: plan.tail]

    number = lax.broadcasted_iota(jnp.int32, (fresh, recomputed), 0)
    key = lax.broadcasted_iota(jnp.int32, (fresh, recomputed), 1)
    for j in range(join):
        seen = jnp.where(key <= j * fresh + number, 0.0, -BIG)
        for head in range(heads):
            mask[j * block + head * fresh : j * block + (head + 1) * fresh, :] = seen
    mask[join * block :, :] = jnp.zeros((plan.tail, recomputed), jnp.float32)

    lane = lax.broadcasted_iota(jnp.int32, (fresh, dim), 1)
    rate = turns_per_step(lax.rem(lane, half), dim)
    signed = jnp.where(lane < half, -rate, rate)

    def places_of(u):
        request = me[0] * requests + u
        column[:join, :fresh] = recomp[request].astype(jnp.float32)
        upright = column[...].T
        for j in range(join):
            inside = jnp.broadcast_to(upright[:fresh, j : j + 1], (fresh, dim))
            places[u * join + j] = inside
            at = inside + float(j * plan.length)
            table[0, u, j * fresh : (j + 1) * fresh, :] = sine_of_turns(at * rate + 0.25)
            table[1, u, j * fresh : (j + 1) * fresh, :] = sine_of_turns(at * signed)

    for load in loads[:3]:
        load.wait()
    plan_work(plan, me, home, spans, work)
    column[...] = jnp.zeros(column.shape, jnp.float32)
    for u in range(requests):
        places_of(u)
    step = lax.broadcasted_iota(jnp.int32, (decode * requests, dim), 0) // requests
    at = (join * plan.length + step).astype(jnp.float32)
    lane = lax.broadcasted_iota(jnp.int32, (decode * requests, dim), 1)
    rate = turns_per_step(lax.rem(lane, half), dim)
    last_cos = sine_of_turns(at * rate + 0.25)
    last_sin = sine_of_turns(at * jnp.where(lane < half, -rate, rate))

    for load in loads[3:]:
        load.wait()

    def queries_of(j):
        rows = slice(j * fresh, (j + 1) * fresh)
        for head in range(heads):
            x = newq[rows, :, head * dim : (head + 1) * dim].astype(jnp.float32)
            flat[head, : fresh * requests, :] = x.reshape(fresh * requests, dim)
        for u in range(requests):
            cosines = table[0, u, rows, :] * scale
            sines = table[1, u, rows, :] * scale
            for head in range(heads):
                y = turn(flat[head, pl.ds(u, fresh, stride=requests), :], cosines, sines)
                q_out[u, pl.ds(j * block + head * fresh, fresh), :] = y.astype(jnp.bfloat16)

    for j in range(join):
        queries_of(j)
    for head in range(heads):
        x = newq[recomputed:, :, head * dim : (head + 1) * dim].astype(jnp.float32)
        y = turn(x.reshape(decode * requests, dim), last_cos, last_sin) * scale
        tails[head * decode * requests : (head + 1) * decode * requests, :] = y
    for u in range(requests):
        y = tails[pl.ds(u, plan.tail, stride=requests), :]
        q_out[u, join * block :, :] = y.astype(jnp.bfloat16)

    x = newkv[:recomputed, :, :].astype(jnp.float32)
    for side in range(2):
        flat[side, : recomputed * requests, :] = x[:, :, side * dim : (side + 1) * dim].reshape(recomputed * requests, dim)
    x = newkv[recomputed:, :, :].astype(jnp.float32)
    last_kv[:, :dim] = turn(x[:, :, :dim].reshape(decode * requests, dim), last_cos, last_sin).astype(
        jnp.bfloat16
    ).astype(jnp.float32)
    last_kv[:, dim:] = x[:, :, dim:].reshape(decode * requests, dim)
    which = lax.rem(lax.broadcasted_iota(jnp.int32, (plan.tail, dim), 0), decode)
    lead = lax.broadcasted_iota(jnp.int32, (plan.tail, dim), 1) == 0

    def fresh_of(u):
        y = turn(flat[0, pl.ds(u, recomputed, stride=requests), :], table[0, u], table[1, u])
        fresh_k[u] = y.T.astype(jnp.bfloat16)
        fresh_v[u] = flat[1, pl.ds(u, recomputed, stride=requests), :].astype(jnp.bfloat16)
        s = jnp.dot(q_out[u], fresh_k[u], preferred_element_type=jnp.float32)
        p = jnp.exp2(s + mask[...])
        acc[u, :, dim:] = p
        acc[u, :, :dim] = jnp.dot(p.astype(jnp.bfloat16), fresh_v[u], preferred_element_type=jnp.float32)
        mine = q_out[u, join * block :, :].astype(jnp.float32)
        for d in range(decode):
            pair = last_kv[pl.ds(d * requests + u, 1), :]
            s = jnp.sum(mine * pair[:, :dim], 1, keepdims=True)
            p = jnp.where(which >= d, jnp.exp2(jnp.broadcast_to(s, which.shape)), 0.0)
            acc[u, join * block :, :dim] += p * pair[:, dim:]
            acc[u, join * block :, dim:] += jnp.where(lead, p, 0.0)

    for u in range(requests):
        fresh_of(u)


def spread_chunk(plan, chunk, values):
    dim, piece = plan.dim, plan.piece
    for first in range(0, chunk.shape[0], piece):
        values[first : first + dim, :] = chunk[first + dim : first + piece, :dim]
        values[first + dim : first + piece, :] = chunk[first + dim : first + piece, dim:]


def shift_keys(plan, chunk, first_token, place, angles, keys):
    dim, piece, fresh = plan.dim, plan.piece, plan.fresh
    half = dim // 2
    wide = lambda x: jnp.concatenate([x] * (piece // dim), 1)
    cosines, sines = wide(angles[:half]), wide(angles[half:])
    place = wide(place)
    for first in range(0, chunk.shape[0], piece):
        columns = slice(first, first + piece)
        a = chunk[first : first + half, :].astype(jnp.float32)
        b = chunk[first + half : first + dim, :].astype(jnp.float32)
        keys[:half, columns] = (a * cosines - b * sines).astype(jnp.bfloat16)
        keys[half:dim, columns] = (b * cosines + a * sines).astype(jnp.bfloat16)
        token = lax.broadcasted_iota(jnp.int32, (fresh, piece), 1) + (first_token + first)
        token = token.astype(jnp.float32)
        keys[dim : dim + fresh, columns] = jnp.where(token > place, -BIG, 0.0).astype(jnp.bfloat16)
        keys[dim + fresh : dim + 2 * fresh, columns] = jnp.where(token == place, -BIG, 0.0).astype(jnp.bfloat16)


def chunk_kernel(plan, order, _work, chunk, places, turns, marks, q, _acc, acc, work, keys, values):
    dim, block, join = plan.dim, plan.block, plan.join
    length = chunk.shape[0]
    keys[dim + 2 * plan.fresh :, :] = jnp.zeros((dim - 2 * plan.fresh, length), jnp.bfloat16)
    spread_chunk(plan, chunk, values)
    base = order * (plan.requests + 1)

    def prepare(n):
        place = work[base + 1 + n]
        shift_keys(plan, chunk, 0, places[place], turns[lax.rem(place, join)], keys)

    def one(n, carry):
        place = work[base + 1 + n]
        u = lax.div(place, join)
        j = place - u * join
        for k in range(join):

            @pl.when(j == k)
            def _():
                count = plan.height - k * block
                left = jnp.concatenate([q[u, k * block :, :], marks[:count, :]], 1)
                s = jnp.dot(left, keys[...], preferred_element_type=jnp.float32)
                prepare(jnp.minimum(n + 1, plan.requests - 1))
                p = jnp.exp2(s)
                parts = [p[:, first : first + dim] for first in range(0, length, dim)]
                while len(parts) > 1:
                    parts = [sum(parts[i : i + 2]) for i in range(0, len(parts), 2)]
                acc[u, k * block :, dim:] += parts[0]
                acc[u, k * block :, :dim] += jnp.dot(
                    p.astype(jnp.bfloat16), values[...], preferred_element_type=jnp.float32
                )

        return carry

    prepare(0)
    lax.fori_loop(0, work[base], one, 0)


def finish_kernel(plan, work, *refs):
    chunks = refs[: plan.slots]
    (places, turns, marks, q, acc, fresh_k, fresh_v, last_kv, out,
     done, flat, tails, joined, keys, values, top, total, peak, sems, load) = refs[plan.slots :]
    dim, fresh, requests, heads, block = plan.dim, plan.fresh, plan.requests, plan.heads, plan.block
    recomputed, decode, join = plan.recomputed, plan.decode, plan.join

    def quotient(a, weight):
        return a * pl.reciprocal(weight, approx=True)

    def tree(join_two, items):
        while len(items) > 1:
            items = [functools.reduce(join_two, items[i : i + 2]) for i in range(0, len(items), 2)]
        return items[0]

    def put(u, j, source, seen):
        weights, quotients = [], []
        for head in range(heads):
            a, weight = source(slice(head * fresh, (head + 1) * fresh))
            o = quotient(a, weight)
            flat[j, head, pl.ds(u, fresh, stride=requests), :] = o
            weights.append(weight)
            quotients.append(o)
        least, most, every = seen
        least = jnp.minimum(least, tree(jnp.minimum, weights))
        most = jnp.maximum(most, tree(jnp.maximum, weights))
        return least, most, every + tree(jnp.add, quotients)

    def put_tail(u, a, weight):
        o = quotient(a, weight)
        tails[pl.ds(u, plan.tail, stride=requests), :] = o
        return weight, weight, o

    def summed(u, start, count):
        a = acc[u, start : start + count, :]
        return a[:, :dim], jnp.sum(a[:, dim:], 1, keepdims=True)

    def write(j):
        rows = pl.ds(j * fresh, fresh)
        for head in range(heads):
            x = flat[j, head, : fresh * requests, :].reshape(fresh, requests, dim)
            done[rows, :, head * dim : (head + 1) * dim] = x.astype(jnp.bfloat16)
        return rows

    def write_tail():
        for head in range(heads):
            x = tails[head * decode * requests : (head + 1) * decode * requests, :]
            done[recomputed:, :, head * dim : (head + 1) * dim] = x.reshape(decode, requests, dim).astype(jnp.bfloat16)

    def send(j):
        rows = pl.ds(j * fresh, fresh) if j < join else pl.ds(recomputed, decode)
        return pltpu.make_async_copy(done.at[rows], out.at[rows], sems.at[j])

    def fits(least, most, every):
        good = (least > 2.0**-60) & (most < 2.0**60) & (every - every == 0.0)
        return jnp.min(jnp.where(good, 1.0, 0.0)) > 0.5

    one, none = jnp.ones((fresh, 1), jnp.float32), jnp.zeros((fresh, dim), jnp.float32)
    clean = (one, one, none)
    ends = [put_tail(u, *summed(u, join * block, plan.tail)) for u in range(requests)]
    ends = [tree(*pair) for pair in zip((jnp.minimum, jnp.maximum, jnp.add), map(list, zip(*ends)))]
    write_tail()
    send(join).start()
    seen = clean
    for j in range(join):
        for u in range(requests):
            source = lambda rows: summed(u, j * block + rows.start, fresh)
            seen = put(u, j, source, seen)
        write(j)
        send(j).start()
    good = fits(*ends) & fits(*seen)
    for j in range(join + 1):
        send(j).wait()

    @pl.when(jnp.logical_not(good))
    def _():
        keys[dim + 2 * fresh :, :] = jnp.zeros((dim - 2 * fresh, plan.length), jnp.bfloat16)

        def fold(rows, s, v):
            before = peak[rows, :]
            now = jnp.maximum(before, jnp.max(s, 1, keepdims=True))
            peak[rows, :] = now
            fade = jnp.exp2(before - now)
            p = jnp.exp2(s - now[:, :1]).astype(jnp.bfloat16)
            total[rows, :] = total[rows, :] * fade + jnp.sum(p.astype(jnp.float32), 1, keepdims=True)
            top[rows, :] = top[rows, :] * fade + jnp.dot(p, v, preferred_element_type=jnp.float32)

        def sums(u, j):
            count = block if j < join else plan.tail
            every = pl.ds(0, count)
            peak[every, :] = jnp.full((count, dim), -3.0e38, jnp.float32)
            top[every, :] = jnp.zeros((count, dim), jnp.float32)
            total[every, :] = jnp.zeros((count, dim), jnp.float32)
            mine = q[u, j * block : j * block + count, :]
            s = jnp.dot(mine, fresh_k[u], preferred_element_type=jnp.float32)
            key = lax.broadcasted_iota(jnp.int32, s.shape, 1)
            row = lax.broadcasted_iota(jnp.int32, s.shape, 0)
            if j < join:
                s = jnp.where(key <= j * fresh + lax.rem(row, fresh), s, -BIG)
            fold(every, s, fresh_v[u])
            for k in range(min(j + 1, join)):
                for order, chunk in enumerate(chunks):

                    @pl.when(work[plan.slots * (requests + 1) + u * join + k] == order)
                    def _():
                        copy = pltpu.make_async_copy(chunk, joined, load.at[0])
                        copy.start()
                        copy.wait()

                spread_chunk(plan, joined, values)
                shift_keys(plan, joined, 0, places[u * join + k], turns[k], keys)
                mark = marks[:count, :] if k == j else marks[block : block + count, :]
                left = jnp.concatenate([mine, mark], 1)
                s = jnp.dot(left, keys[...], preferred_element_type=jnp.float32)
                fold(every, s, values[...])
            if j == join:
                which = lax.rem(lax.broadcasted_iota(jnp.int32, (count, dim), 0), decode)
                for d in range(decode):
                    pair = last_kv[pl.ds(d * requests + u, 1), :]
                    s = jnp.sum(mine.astype(jnp.float32) * pair[:, :dim], 1, keepdims=True)
                    s = jnp.where(which >= d, s, -BIG)
                    before = peak[every, :]
                    now = jnp.maximum(before, s)
                    peak[every, :] = now
                    p = jnp.exp2(s - now)
                    total[every, :] = total[every, :] * jnp.exp2(before - now) + p
                    top[every, :] = top[every, :] * jnp.exp2(before - now) + p * pair[:, dim:]

        for j in range(join + 1):

            def again(u, carry):
                sums(u, j)
                if j < join:
                    put(u, j, lambda rows: (top[rows, :], total[rows, :1]), clean)
                else:
                    put_tail(u, top[: plan.tail, :], total[: plan.tail, :1])
                return carry

            lax.fori_loop(0, requests, again, 0)
            if j < join:
                write(j)
            else:
                write_tail()
            copy = send(j)
            copy.start()
            copy.wait()


def local(span_kv, span_home, request_spans, recomp_pos, new_q, new_kv):
    groups = lax.axis_size("store") // KV_HEADS
    me = (lax.axis_index("store") // KV_HEADS).reshape(1).astype(jnp.int32)
    plan = Plan(span_kv, request_spans, recomp_pos, new_q, groups)
    dim, join, requests = plan.dim, plan.join, plan.requests
    vmem = pl.BlockSpec(memory_space=pltpu.VMEM)
    smem = pl.BlockSpec(memory_space=pltpu.SMEM)
    anywhere = pl.BlockSpec(memory_space=pl.ANY)
    params = lambda mib: pltpu.CompilerParams(vmem_limit_bytes=mib * MIB)
    inside = lambda x: pltpu.with_memory_space_constraint(x, pltpu.VMEM)
    outside = lambda x: pltpu.with_memory_space_constraint(x, pltpu.HBM)
    cost = lambda us: pl.CostEstimate(flops=int(us * 2e7), bytes_accessed=0, transcendentals=0)

    packed = pl.pallas_call(
        functools.partial(pack_kernel, plan),
        out_shape=[pltpu.VMEM((plan.length, 2 * dim), jnp.bfloat16)] * plan.per_group,
        in_specs=[vmem],
        out_specs=[vmem] * plan.per_group,
        compiler_params=params(6),
        cost_estimate=cost(1.0),
        name="pack",
    )(span_kv)

    buffers = {(0, c): x for c, x in enumerate(packed)}

    for after in plan.order[1:3]:
        for c in range(plan.per_group):
            buffers[after, c] = shifted(packed[c], "store", plan.way(after))

    spans = request_spans.T

    work_type = pltpu.SMEM((plan.slots * (requests + 1) + requests * join,), jnp.int32)
    acc_type = pltpu.VMEM((requests, plan.height, 2 * dim), jnp.float32)
    q, acc, places, turns, marks, fresh_k, fresh_v, last_kv, work = pl.pallas_call(
        functools.partial(prepare_kernel, plan),
        out_shape=[
            pltpu.VMEM((requests, plan.height, dim), jnp.bfloat16),
            acc_type,
            pltpu.VMEM((requests * join, plan.fresh, dim), jnp.float32),
            pltpu.VMEM((join, dim, dim), jnp.float32),
            pltpu.VMEM((plan.height, dim), jnp.bfloat16),
            pltpu.VMEM((requests, dim, plan.recomputed), jnp.bfloat16),
            pltpu.VMEM((requests, plan.recomputed, dim), jnp.bfloat16),
            pltpu.VMEM((plan.decode * requests, 2 * dim), jnp.float32),
            work_type,
        ],
        in_specs=[smem] + [anywhere] * 5,
        out_specs=[vmem] * 8 + [smem],
        scratch_shapes=[
            pltpu.SMEM(span_home.shape, jnp.int32),
            pltpu.SMEM(spans.shape, jnp.int32),
            pltpu.VMEM((plan.rows, requests, new_q.shape[2]), jnp.bfloat16),
            pltpu.VMEM((plan.rows, requests, 2 * dim), jnp.bfloat16),
            pltpu.VMEM(recomp_pos.shape, jnp.int32),
            pltpu.VMEM((2, requests, plan.recomputed, dim), jnp.float32),
            pltpu.VMEM((plan.heads, (plan.recomputed + 1) * requests, dim), jnp.float32),
            pltpu.VMEM(((plan.tail + 1) * requests, dim), jnp.float32),
            pltpu.VMEM((dim, dim), jnp.float32),
            pltpu.VMEM((plan.height, plan.recomputed), jnp.float32),
            pltpu.SemaphoreType.DMA((5,)),
        ],
        compiler_params=params(20),
        cost_estimate=cost(6.0),
        name="prepare",
    )(me, *map(outside, [span_home, spans, new_q.transpose(1, 0, 2), new_kv.transpose(1, 0, 2), recomp_pos]))
    scalar = lambda x: pltpu.with_memory_space_constraint(x, pltpu.SMEM)

    def take(order, chunk, acc, work):
        return pl.pallas_call(
            functools.partial(chunk_kernel, plan, order),
            out_shape=[acc_type, work_type],
            in_specs=[smem] + [vmem] * 6,
            out_specs=[vmem, smem],
            input_output_aliases={6: 0, 0: 1},
            scratch_shapes=[
                pltpu.VMEM((2 * dim, plan.length), jnp.bfloat16),
                pltpu.VMEM((plan.length, dim), jnp.bfloat16),
            ],
            compiler_params=params(12),
            cost_estimate=cost(2.5),
            name="chunk",
        )(scalar(work), *map(inside, [chunk, places, turns, marks, q, acc]))

    def onward(distance, c, work):
        for after in plan.order:
            if distance > 0 and after > 0 and plan.source(after) == distance:
                buffers[distance, c], work = lax.optimization_barrier((buffers[distance, c], work))
                buffers[after, c] = shifted(buffers[distance, c], "store", plan.way(after))
        return work

    chunks = [(distance, c) for distance in plan.order for c in range(plan.per_group)]
    first = plan.per_group
    if groups > 1:
        work = onward(*chunks[first], work)
    for order, (distance, c) in enumerate(chunks):
        acc, work = take(order, buffers[distance, c], acc, work)
        if order > first:
            work = onward(distance, c, work)
    buffers = [buffers[chunk] for chunk in chunks]

    out = pl.pallas_call(
        functools.partial(finish_kernel, plan),
        out_shape=jax.ShapeDtypeStruct((plan.rows, requests, new_q.shape[2]), jnp.bfloat16),
        in_specs=[smem] + [anywhere] * len(buffers) + [vmem] * 8,
        out_specs=anywhere,
        scratch_shapes=[
            pltpu.VMEM((plan.rows, requests, new_q.shape[2]), jnp.bfloat16),
            pltpu.VMEM((join, plan.heads, (plan.fresh + 1) * requests, dim), jnp.float32),
            pltpu.VMEM(((plan.tail + 1) * requests, dim), jnp.float32),
            pltpu.VMEM((plan.length, 2 * dim), jnp.bfloat16),
            pltpu.VMEM((2 * dim, plan.length), jnp.bfloat16),
            pltpu.VMEM((plan.length, dim), jnp.bfloat16),
            pltpu.VMEM((plan.block, dim), jnp.float32),
            pltpu.VMEM((plan.block, dim), jnp.float32),
            pltpu.VMEM((plan.block, dim), jnp.float32),
            pltpu.SemaphoreType.DMA((join + 1,)),
            pltpu.SemaphoreType.DMA((1,)),
        ],
        compiler_params=params(24),
        cost_estimate=cost(3.0),
        name="finish",
    )(scalar(work), *buffers, *map(inside, [places, turns, marks, q, acc, fresh_k, fresh_v, last_kv]))
    return out.transpose(1, 0, 2)


def solution(mesh):
    return jax.shard_map(
        local,
        mesh=mesh,
        in_specs=(
            P(("groups", "store"), None, None),
            P("groups"),
            P("groups", None),
            P("groups", None, None),
            P(("groups", "store"), None, None),
            P(("groups", "store"), None, None),
        ),
        out_specs=P(("groups", "store"), None, None),
        check_vma=False,
    )
```
